32 devices in a mesh: groups: 2 (over x), cols: 16 (over z, y, core).
Axes of the slice: x: 2, y: 2, z: 4, core: 2. Of those that a mesh axis runs over, the one named last changes fastest.
Arguments:
- hidden: bfloat16 [512, 14848], P(('groups', 'cols')), parts along dimension 0, may hold values from -6 to 6
- down_weight: bfloat16 [14848, 4096], P('cols'), may hold values from -0.046875 to 0.046875
- delta_values: bfloat16 [64, 186, 128, 128], P('cols'), may hold values from -0.119628906 to 0.119628906
- block_ids: int32 [64, 186], P('cols'), may hold values from 0 to 3711, as said below
- variant_slot: int32 [64], replicated, may hold values from 0 to 63, each once
- row_variant: int32 [512, 1], P(('groups', 'cols')), parts along dimension 0, may hold values from 0 to 63; in each aligned block of 256 rows (0 to 255, 256 to 511, ...) at most 8 rows name the same one
Outputs:
- mixed_out: bfloat16 [512, 4096], P(('groups', 'cols')), parts along dimension 0
The draws below stay inside these ranges and needn't reach their ends.
There are 2 independent parts, one for each index of `groups`. The reference program is written for one: setup_inputs(seed, part) draws one part's arguments, and reference() takes and returns one part's arrays. A program takes and returns all parts, laid end to end along the dimension named above; an argument that names none is the same for every part. Nothing has to cross between parts.
Inputs may be any that keep to these rules, and one draw needn't show every extreme that they name: `block_ids`: the 186 entries of one slot are distinct. `row_variant`: at most 8 rows name the same variant, every variant is named by some row, and in every draw some variant is named by exactly 8 rows. `variant_slot`: each slot holds exactly one variant.
All inputs are finite; a program needn't handle non-finite values.
Results may differ from the reference program's by a relative error of at most 0.0055.
Values may be sent and summed in bfloat16 or wider, within the bound.
No kernel may reach another device: no remote copies, remote signals or barrier semaphores. Data moves between devices by JAX's collectives and lax.ppermute only.
A program may use at most 128 MiB of HBM per device.

```python
import math
import jax
import jax.numpy as jnp
import numpy as np
from jax import lax

D = 4096
F = 14848
BLK = 128
NB = 186
VARIANTS = 64
ROWS = 256
ROW_CAP = 8


def draw_block_ids(key, part):
    key = jax.random.fold_in(key, 5)
    keys = jax.random.split(key, VARIANTS)
    total = F // BLK * (D // BLK)

    def one_list(single):
        return jax.random.permutation(single, total)[:NB]
    return jax.vmap(one_list)(keys).astype(jnp.int32)


def block_levels(stream_key, dims, cuts, smallest, high):
    loudness = 1.0
    for position, parts in cuts:
        draws = jax.random.uniform(jax.random.fold_in(jax.random.fold_in(stream_key, 6), position), (parts,), jnp.float32, smallest / len(cuts), high / len(cuts))
        loudness = loudness * jnp.repeat(jnp.exp(draws), dims[position] // parts).reshape((-1,) + (1,) * (len(dims) - 1 - position))
    return loudness


def deal_out(rng, own, number, rows, count, top, limit, slope):
    order = jax.random.permutation(rng, count)
    packed, usual = portions_of(count, rows * top, limit, slope, True), portions_of(count, rows * top, limit, slope, False)
    places = jnp.arange(count)

    def named(sizes, turn):
        used = int((sizes > 0).sum())
        fixed = max(1, used // 4)
        passed = fixed + (places - fixed + turn * (used - fixed)) % max(1, count - fixed)
        return jnp.zeros((count,), jnp.int32).at[order[jnp.where(places < fixed, places, passed)]].set(jnp.asarray(sizes, jnp.int32))

    sizes = jnp.where(number % 4 == 0, named(packed, number // 4), named(usual, number - number // 4 - 1))
    mixed = jax.random.permutation(jax.random.fold_in(own, 3), count)
    donor, receiver = mixed[0:count // 2 * 2:2], mixed[1:count // 2 * 2:2]
    slack = jnp.minimum(sizes[donor] - 1, limit - sizes[receiver]) // 2
    slack = jnp.where((donor == order[0]) | (receiver == order[0]) | (sizes[receiver] == 0), 0, jnp.maximum(slack, 0))
    passed = jax.random.randint(jax.random.fold_in(own, 4), (count // 2,), 0, 1 << 20) % (slack + 1)
    sizes = sizes.at[donor].add(-passed).at[receiver].add(passed)
    items = jnp.searchsorted(jnp.cumsum(sizes), jnp.arange(rows * top), side="right").astype(jnp.int32)
    listing = items.reshape(top, rows).T
    listing = listing[jax.random.permutation(jax.random.fold_in(own, 1), rows)]
    turn = jax.random.randint(jax.random.fold_in(own, 2), (rows, 1), 0, top)
    return jnp.take_along_axis(listing, (jnp.arange(top)[None, :] + turn) % top, axis=1)


def portions_of(amount, total, most, lean, full):
    portions = [(1 << 20) // math.isqrt(rank ** lean) + 1 for rank in range(1, amount + 1)]
    largest = most if full else min(most, max(-(-total // amount), total * portions[0] // sum(portions)))
    least = 1 if total - largest >= amount - 1 else 0
    holding, surplus = [largest] + [least] * (amount - 1), total - largest - least * (amount - 1)
    while surplus > 0:
        candidates = [i for i in range(1, amount) if holding[i] < largest] or [i for i in range(1, amount) if holding[i] < most]
        whole, remaining = sum([portions[i] for i in candidates]), surplus
        for i in candidates:
            extra = min(most - holding[i], max(1, remaining * portions[i] // whole), surplus)
            holding[i] = holding[i] + extra
            surplus = surplus - extra
    return np.array(holding)


def scatter_about(stream_key, shape, spread, bound, shards=(), held_as=jnp.bfloat16):
    factor_of = block_levels(stream_key, shape, shards, -0.22, 0.18) if shards else 1.0
    drawn = jax.random.normal(stream_key, shape, jnp.float32) * spread * factor_of
    return jnp.minimum(jnp.maximum(drawn, -bound), bound).astype(held_as)


def setup_inputs(seed: int = 0, part: int = 0) -> dict:
    arg_keys = jax.random.split(jax.random.key(seed), 7)
    part_splits = jax.random.split(jax.random.fold_in(arg_keys[6], part), 7)
    hidden = scatter_about(part_splits[0], (ROWS, F), 1.0, 6.0, ((0, 16),))
    down_weight = scatter_about(arg_keys[1], (F, D), F ** -0.5, 0.046875, ((0, 16),))
    delta_values = scatter_about(arg_keys[2], (VARIANTS, NB, BLK, BLK), 0.02, 0.119628906, ((0, 16),))
    block_ids = draw_block_ids(jax.random.fold_in(arg_keys[6], 71), part)
    variant_slot = jax.random.permutation(arg_keys[4], VARIANTS).astype(jnp.int32)
    row_variant_keys = jax.random.split(jax.random.fold_in(part_splits[5], 1), ROWS // ROWS)
    row_variant_turns = jax.random.permutation(jax.random.fold_in(part_splits[5], 3), ROWS // ROWS)
    row_variant = jax.vmap(lambda own, number: deal_out(jax.random.fold_in(part_splits[5], 2), own, number, ROWS, VARIANTS, 1, ROW_CAP, 2))(row_variant_keys, row_variant_turns).reshape((ROWS, 1))
    return dict(hidden=hidden, down_weight=down_weight, delta_values=delta_values, block_ids=block_ids, variant_slot=variant_slot, row_variant=row_variant)


def reference(hidden, down_weight, delta_values, block_ids, variant_slot, row_variant):
    base = jnp.dot(hidden, down_weight, preferred_element_type=jnp.float32)
    slot_of = variant_slot[row_variant[:, 0]].astype(jnp.int32)
    d_blocks = D // BLK

    def one_row(item):
        row_vector, slot_index = item
        values = delta_values[slot_index].astype(jnp.float32)
        block_list = block_ids[slot_index]
        pieces = row_vector.reshape(F // BLK, BLK)[block_list // d_blocks].astype(jnp.float32)
        products = jnp.einsum("nk,nkj->nj", pieces, values)
        summed = jnp.zeros((d_blocks, BLK), jnp.float32).at[block_list % d_blocks].add(products)
        return summed.reshape(D).astype(jnp.bfloat16)

    delta = lax.map(one_row, (hidden, slot_of))
    return (base + delta.astype(jnp.float32)).astype(jnp.bfloat16)
```

```python
import functools

import jax
import jax.numpy as jnp
from jax import lax
from jax.experimental import pallas as pl
from jax.experimental.pallas import tpu as pltpu
from jax.sharding import PartitionSpec as P

LANES = 128
BF16 = jnp.bfloat16
F32 = jnp.float32


def windows(width_f, peers):
    share = width_f // peers
    most = max((s * share) % LANES for s in range(peers))
    window = -(-(share + most) // LANES) * LANES
    if window == share:
        window += LANES
    last = (width_f - window) // LANES
    starts = [min(s * share // LANES, last) for s in range(peers)]
    return share, window, last, starts


def params(**kw):
    return pltpu.CompilerParams(vmem_limit_bytes=48 * 1024 * 1024, **kw)


def lane_iota(rows, lanes):
    return lax.broadcasted_iota(jnp.int32, (rows, lanes), 1)


def split_kernel(plan, h_ref, id_ref, o_ref):
    share, window, _, starts = plan
    rows = h_ref.shape[0]
    lane = lane_iota(rows, window)
    ids = id_ref[...].astype(F32)
    for s, b in enumerate(starts):
        shift = s * share - b * LANES
        piece = h_ref[:, b * LANES : b * LANES + window].astype(F32)
        keep = (lane >= shift) & (lane < shift + share)
        spare = (shift + share) % window
        piece = jnp.where(keep, piece, jnp.where(lane == spare, ids, 0.0))
        o_ref[s] = piece.astype(BF16)


def own_shift(plan):
    share, _, last, _ = plan
    start = lax.axis_index("cols") * share
    return start - jnp.minimum(start // LANES, last) * LANES


def route_kernel(plan, capacity, shift_ref, x_ref, slot_ref, o_ref, place_ref):
    share, window, _, _ = plan
    peers, row_dev, _ = x_ref.shape
    rows = peers * row_dev
    variants = slot_ref.shape[1]
    slots = variants * capacity
    shift = shift_ref[0]
    x = x_ref[...].reshape(rows, window).astype(F32)
    lane = lane_iota(rows, window)
    spare = lax.rem(shift + share, window)
    ids = jnp.sum(jnp.where(lane == spare, x, 0.0), axis=1, keepdims=True)
    data = jnp.where((lane >= shift) & (lane < shift + share), x, 0.0).astype(BF16)
    onehot = ids.astype(jnp.int32) == lane_iota(rows, variants)
    onehot_f = jnp.where(onehot, 1.0, 0.0)
    row_i = lax.broadcasted_iota(jnp.int32, (rows, rows), 0)
    row_j = lane_iota(rows, rows)
    earlier = jnp.where(row_j < row_i, 1.0, 0.0).astype(BF16)
    before = jnp.dot(earlier, onehot_f.astype(BF16), preferred_element_type=F32)
    rank = jnp.sum(before * onehot_f, axis=1, keepdims=True)
    slot_of = jnp.sum(onehot_f * slot_ref[...].astype(F32), axis=1, keepdims=True)
    place = slot_of * capacity + rank
    place_ref[...] = place.astype(jnp.int32)
    across = jnp.sum(jnp.where(row_i == row_j, place, 0.0), axis=0, keepdims=True)
    pick = across.astype(jnp.int32) == lax.broadcasted_iota(jnp.int32, (slots, rows), 0)
    pick = jnp.where(pick, 1.0, 0.0).astype(BF16)
    filled = jnp.dot(pick, data, preferred_element_type=F32).astype(BF16)
    o_ref[...] = filled.reshape(o_ref.shape)


def base_kernel(plan, scal_ref, x_ref, w_ref, keep_ref, send_ref, mine_ref):
    share, window, _, _ = plan
    peers, row_dev, _ = x_ref.shape
    half = peers // 2 * row_dev

    @pl.when(pl.program_id(0) == 0)
    def _():
        bit = scal_ref[1]
        for side in (0, 1):
            which = bit if side == 0 else 1 - bit
            for q in range(peers // 2):
                piece = x_ref[2 * q + which].astype(F32)
                piece = pltpu.roll(piece, window - scal_ref[0], 1)
                mine_ref[side, q * row_dev : (q + 1) * row_dev] = piece[:, :share].astype(BF16)

    w = w_ref[...]
    keep = jnp.dot(mine_ref[0], w, preferred_element_type=F32)
    keep_ref[...] = keep.reshape(keep_ref.shape)
    send = jnp.dot(mine_ref[1], w, preferred_element_type=F32)
    send_ref[...] = send.astype(BF16).reshape(send_ref.shape)


def delta_kernel(plan, d_blocks, ids_ref, x_ref, v_ref, o_ref, rows_ref, acc_ref):
    _, window, _, starts = plan
    local_var, f_blocks, capacity, _ = rows_ref.shape
    group = v_ref.shape[1]
    var, step = pl.program_id(0), pl.program_id(1)

    @pl.when((var == 0) & (step == 0))
    def _():
        acc_ref[...] = jnp.zeros_like(acc_ref)
        done = set()
        for s, b in enumerate(starts):
            for k in range(window // LANES):
                tile = x_ref[s, :, k * LANES : (k + 1) * LANES].astype(F32)
                for v in range(local_var):
                    part = tile[v * capacity : (v + 1) * capacity]
                    if b + k in done:
                        part = part + rows_ref[v, b + k]
                    rows_ref[v, b + k] = part
                done.add(b + k)

    places, products = [], []
    for n in range(group):
        block = ids_ref[var, step * group + n]
        lhs = rows_ref[var, lax.div(block, d_blocks)].astype(BF16)
        products.append(jnp.dot(lhs, v_ref[0, n], preferred_element_type=F32))
        places.append(lax.rem(block, d_blocks))
    for j, product in zip(places, products):
        acc_ref[var, j] += product

    @pl.when((var == pl.num_programs(0) - 1) & (step == pl.num_programs(1) - 1))
    def _():
        for j in range(d_blocks):
            whole = jnp.concatenate([acc_ref[v, j] for v in range(local_var)], axis=0)
            if len(o_ref.shape) == 3:
                per = o_ref.shape[2] // LANES
                k = j % per
                o_ref[j // per, :, k * LANES : (k + 1) * LANES] = whole.astype(BF16)
            else:
                o_ref[:, j * LANES : (j + 1) * LANES] = whole.astype(BF16)


def pick_kernel(place_ref, c_ref, o_ref):
    peers, per_owner, cols = c_ref.shape
    slots = peers * per_owner
    rows = place_ref.shape[0]
    pick = place_ref[...] == lane_iota(rows, slots)
    pick = jnp.where(pick, 1.0, 0.0).astype(BF16)
    found = jnp.dot(pick, c_ref[...].reshape(slots, cols), preferred_element_type=F32)
    o_ref[...] = found.astype(BF16).reshape(o_ref.shape)


def split_factor(count, most):
    return max(g for g in range(1, most + 1) if count % g == 0)


def body(hidden, down_weight, delta_values, block_ids, variant_slot, row_variant):
    peers = lax.axis_size("cols")
    me = lax.axis_index("cols")
    row_dev, width_f = hidden.shape
    width_d = down_weight.shape[1]
    local_var, count, block_size, _ = delta_values.shape
    variants = variant_slot.shape[0]
    all_rows = row_dev * peers
    capacity = 2 * all_rows // variants
    d_blocks = width_d // block_size
    f_blocks = width_f // block_size
    local_slots = local_var * capacity
    plan = windows(width_f, peers)
    share, window, _, _ = plan
    half = peers // 2
    slice_d = width_d // peers

    scal = jnp.stack([own_shift(plan), me % 2]).astype(jnp.int32)
    smem = pl.BlockSpec(memory_space=pltpu.SMEM)

    outgoing = pl.pallas_call(
        functools.partial(split_kernel, plan),
        out_shape=jax.ShapeDtypeStruct((peers, row_dev, window), BF16),
        compiler_params=params(),
        name="split_rows",
    )(hidden, row_variant)
    x = lax.all_to_all(outgoing, "cols", 0, 0)

    slots, place = pl.pallas_call(
        functools.partial(route_kernel, plan, capacity),
        out_shape=(
            jax.ShapeDtypeStruct((peers, local_slots, window), BF16),
            jax.ShapeDtypeStruct((all_rows, 1), jnp.int32),
        ),
        in_specs=[smem, pl.BlockSpec(memory_space=pltpu.VMEM), pl.BlockSpec(memory_space=pltpu.VMEM)],
        compiler_params=params(),
        name="route",
    )(scal, x, variant_slot.reshape(1, variants))
    arrived = lax.all_to_all(slots, "cols", 0, 0)

    tile = min(512, width_d)
    keep, send = pl.pallas_call(
        functools.partial(base_kernel, plan),
        grid=(width_d // tile,),
        out_shape=(
            jax.ShapeDtypeStruct((half, row_dev, width_d), F32),
            jax.ShapeDtypeStruct((half, row_dev, width_d), BF16),
        ),
        in_specs=[
            smem,
            pl.BlockSpec((peers, row_dev, window), lambda t: (0, 0, 0)),
            pl.BlockSpec((share, tile), lambda t: (0, t)),
        ],
        out_specs=(
            pl.BlockSpec((half, row_dev, tile), lambda t: (0, 0, t)),
            pl.BlockSpec((half, row_dev, tile), lambda t: (0, 0, t)),
        ),
        scratch_shapes=[pltpu.VMEM((2, all_rows // 2, share), BF16)],
        compiler_params=params(),
        cost_estimate=pl.CostEstimate(
            flops=2 * all_rows * share * width_d,
            bytes_accessed=2 * share * width_d + 6 * all_rows // 2 * width_d,
            transcendentals=0,
        ),
        name="base",
    )(scal, x, down_weight)
    step = 1
    while True:
        got = lax.ppermute(send, "cols", [(i, i ^ step) for i in range(peers)])
        total = keep + got.astype(F32)
        step *= 2
        if step == peers:
            break
        bit = (me // step) % 2
        total = total.reshape(total.shape[0] // 2, 2, row_dev, width_d)
        keep = lax.dynamic_index_in_dim(total, bit, 1, keepdims=False)
        send = lax.dynamic_index_in_dim(total, 1 - bit, 1, keepdims=False).astype(BF16)
    summed = total.reshape(row_dev, width_d)

    group = split_factor(count, 64)
    aligned = slice_d % LANES == 0
    shape = (peers, local_slots, slice_d) if aligned else (local_slots, width_d)
    deltas = pl.pallas_call(
        functools.partial(delta_kernel, plan, d_blocks),
        grid_spec=pltpu.PrefetchScalarGridSpec(
            num_scalar_prefetch=1,
            grid=(local_var, count // group),
            in_specs=[
                pl.BlockSpec((peers, local_slots, window), lambda v, s, ids: (0, 0, 0)),
                pl.BlockSpec((1, group, block_size, block_size), lambda v, s, ids: (v, s, 0, 0)),
            ],
            out_specs=pl.BlockSpec(shape, lambda v, s, ids: (0,) * len(shape)),
            scratch_shapes=[
                pltpu.VMEM((local_var, f_blocks, capacity, block_size), F32),
                pltpu.VMEM((local_var, d_blocks, capacity, block_size), F32),
            ],
        ),
        out_shape=jax.ShapeDtypeStruct(shape, BF16),
        compiler_params=params(),
        cost_estimate=pl.CostEstimate(
            flops=2 * local_slots * count * block_size * block_size,
            bytes_accessed=2 * local_var * count * block_size * block_size,
            transcendentals=0,
        ),
        name="delta",
    )(block_ids, arrived, delta_values)
    if not aligned:
        deltas = deltas.reshape(local_slots, peers, slice_d).transpose(1, 0, 2)
    columns = lax.all_to_all(deltas, "cols", 0, 0)
    by_row = pl.pallas_call(
        pick_kernel,
        out_shape=jax.ShapeDtypeStruct((peers, row_dev, slice_d), BF16),
        compiler_params=params(),
        name="pick",
    )(place, columns)
    own = lax.all_to_all(by_row, "cols", 0, 0)
    own = own.transpose(1, 0, 2).reshape(row_dev, width_d)
    return (summed + own.astype(F32)).astype(BF16)


def solution(mesh):
    return jax.shard_map(
        body,
        mesh=mesh,
        in_specs=(
            P(("groups", "cols"), None),
            P("cols", None),
            P("cols", None, None, None),
            P("cols", None),
            P(),
            P(("groups", "cols"), None),
        ),
        out_specs=P(("groups", "cols"), None),
        check_vma=False,
    )
```

```python
import functools

import jax
import jax.numpy as jnp
from jax import lax
from jax.experimental import pallas as pl
from jax.experimental.pallas import tpu as pltpu
from jax.sharding import PartitionSpec as P

LANES = 128
BF16 = jnp.bfloat16
F32 = jnp.float32


def windows(width_f, peers):
    share = width_f // peers
    most = max((s * share) % LANES for s in range(peers))
    window = -(-(share + most) // LANES) * LANES
    if window == share:
        window += LANES
    last = (width_f - window) // LANES
    starts = [min(s * share // LANES, last) for s in range(peers)]
    return share, window, last, starts


def params(mib=16):
    return pltpu.CompilerParams(vmem_limit_bytes=mib * 1024 * 1024)


def lane_iota(rows, lanes):
    return lax.broadcasted_iota(jnp.int32, (rows, lanes), 1)


def split_kernel(plan, h_ref, id_ref, o_ref):
    share, window, _, starts = plan
    rows = h_ref.shape[0]
    lane = lane_iota(rows, window)
    ids = id_ref[...].astype(F32)
    for s, b in enumerate(starts):
        shift = s * share - b * LANES
        piece = h_ref[:, b * LANES : b * LANES + window].astype(F32)
        keep = (lane >= shift) & (lane < shift + share)
        spare = (shift + share) % window
        piece = jnp.where(keep, piece, jnp.where(lane == spare, ids, 0.0))
        o_ref[s] = piece.astype(BF16)


def own_shift(plan):
    share, _, last, _ = plan
    start = lax.axis_index("cols") * share
    return start - jnp.minimum(start // LANES, last) * LANES


def route_kernel(plan, capacity, shift_ref, x_ref, slot_ref, o_ref, place_ref):
    share, window, _, _ = plan
    peers, row_dev, _ = x_ref.shape
    rows = peers * row_dev
    variants = slot_ref.shape[1]
    slots = variants * capacity
    shift = shift_ref[0]
    x = x_ref[...].reshape(rows, window).astype(F32)
    lane = lane_iota(rows, window)
    spare = lax.rem(shift + share, window)
    ids = jnp.sum(jnp.where(lane == spare, x, 0.0), axis=1, keepdims=True)
    data = jnp.where((lane >= shift) & (lane < shift + share), x, 0.0).astype(BF16)
    onehot = ids.astype(jnp.int32) == lane_iota(rows, variants)
    onehot_f = jnp.where(onehot, 1.0, 0.0)
    row_i = lax.broadcasted_iota(jnp.int32, (rows, rows), 0)
    row_j = lane_iota(rows, rows)
    earlier = jnp.where(row_j < row_i, 1.0, 0.0).astype(BF16)
    before = jnp.dot(earlier, onehot_f.astype(BF16), preferred_element_type=F32)
    rank = jnp.sum(before * onehot_f, axis=1, keepdims=True)
    slot_of = jnp.sum(onehot_f * slot_ref[...].astype(F32), axis=1, keepdims=True)
    place = slot_of * capacity + rank
    place_ref[...] = place.astype(jnp.int32)
    across = jnp.sum(jnp.where(row_i == row_j, place, 0.0), axis=0, keepdims=True)
    pick = across.astype(jnp.int32) == lax.broadcasted_iota(jnp.int32, (slots, rows), 0)
    pick = jnp.where(pick, 1.0, 0.0).astype(BF16)
    filled = jnp.dot(pick, data, preferred_element_type=F32).astype(BF16)
    o_ref[...] = filled.reshape(o_ref.shape)


def base_kernel(plan, scal_ref, x_ref, w_ref, keep_ref, send_ref, mine_ref):
    share, window, _, _ = plan
    peers, row_dev, _ = x_ref.shape
    half = peers // 2 * row_dev

    @pl.when(pl.program_id(0) == 0)
    def _():
        bit = scal_ref[1]
        for side in (0, 1):
            which = bit if side == 0 else 1 - bit
            for q in range(peers // 2):
                piece = x_ref[2 * q + which].astype(F32)
                piece = pltpu.roll(piece, window - scal_ref[0], 1)
                at = side * half + q * row_dev
                mine_ref[at : at + row_dev] = piece[:, :share].astype(BF16)

    both = jnp.dot(mine_ref[...], w_ref[...], preferred_element_type=F32)
    keep_ref[...] = both[:half].reshape(keep_ref.shape)
    send_ref[...] = both[half:].astype(BF16).reshape(send_ref.shape)


def delta_kernel(plan, d_blocks, group, ids_ref, x_ref, v_hbm, o_ref, rows_ref, acc_ref, held_ref, sems):
    _, window, _, starts = plan
    local_var, f_blocks, capacity, _ = rows_ref.shape
    chunks, _, size, _ = held_ref.shape
    per = chunks // local_var

    def fetch(c):
        source = v_hbm.at[c // per, pl.ds((c % per) * group, group)]
        return pltpu.make_async_copy(source, held_ref.at[c], sems.at[c])

    for c in range(chunks):
        fetch(c).start()

    acc_ref[...] = jnp.zeros_like(acc_ref)
    done = set()
    for s, b in enumerate(starts):
        for k in range(window // LANES):
            tile = x_ref[s, :, k * LANES : (k + 1) * LANES].astype(F32)
            for v in range(local_var):
                part = tile[v * capacity : (v + 1) * capacity]
                if b + k in done:
                    part = part + rows_ref[v, b + k]
                rows_ref[v, b + k] = part
            done.add(b + k)

    zeros = jnp.zeros((capacity, size), F32)

    def one_chunk(c, carry):
        var = lax.div(c, per)
        first = lax.rem(c, per) * group
        pltpu.make_async_copy(
            v_hbm.at[var, pl.ds(first, group)], held_ref.at[c], sems.at[c]
        ).wait()
        sums = []
        for n in range(0, group, 2):
            blocks = [ids_ref[var, first + m] for m in range(n, min(n + 2, group))]
            lhs = [rows_ref[var, lax.div(block, d_blocks)] for block in blocks]
            if len(blocks) == 2:
                upper = jnp.concatenate([lhs[0], zeros], axis=1)
                lower = jnp.concatenate([zeros, lhs[1]], axis=1)
                left = jnp.concatenate([upper, lower], axis=0).astype(BF16)
                right = held_ref[c, n : n + 2].reshape(2 * size, size)
            else:
                left = lhs[0].astype(BF16)
                right = held_ref[c, n]
            product = jnp.dot(left, right, preferred_element_type=F32)
            for q, block in enumerate(blocks):
                part = product[q * capacity : (q + 1) * capacity]
                sums.append((lax.rem(block, d_blocks), part))
        for column, part in sums:
            acc_ref[var, column] += part
        return carry

    lax.fori_loop(0, chunks, one_chunk, 0)
    for j in range(d_blocks):
        whole = jnp.concatenate([acc_ref[v, j] for v in range(local_var)], axis=0)
        if len(o_ref.shape) == 3:
            per_peer = o_ref.shape[2] // LANES
            k = j % per_peer
            o_ref[j // per_peer, :, k * LANES : (k + 1) * LANES] = whole.astype(BF16)
        else:
            o_ref[:, j * LANES : (j + 1) * LANES] = whole.astype(BF16)


def pick_kernel(place_ref, c_ref, o_ref):
    peers, per_owner, cols = c_ref.shape
    slots = peers * per_owner
    rows = place_ref.shape[0]
    pick = place_ref[...] == lane_iota(rows, slots)
    pick = jnp.where(pick, 1.0, 0.0).astype(BF16)
    found = jnp.dot(pick, c_ref[...].reshape(slots, cols), preferred_element_type=F32)
    o_ref[...] = found.astype(BF16).reshape(o_ref.shape)


def halve_kernel(bit_ref, keep_ref, got_ref, next_ref, send_ref):
    bit = bit_ref[0]
    for q in range(next_ref.shape[0]):
        mine, other = 2 * q + bit, 2 * q + 1 - bit
        next_ref[q] = keep_ref[mine] + got_ref[mine].astype(F32)
        send_ref[q] = (keep_ref[other] + got_ref[other].astype(F32)).astype(BF16)


def finish_kernel(keep_ref, got_ref, own_ref, o_ref):
    peers, _, cols = own_ref.shape
    base = keep_ref[0] + got_ref[0].astype(F32)
    if cols % LANES == 0:
        for s in range(peers):
            at = slice(s * cols, (s + 1) * cols)
            o_ref[:, at] = (base[:, at] + own_ref[s].astype(F32)).astype(BF16)
    else:
        own = jnp.concatenate([own_ref[s].astype(F32) for s in range(peers)], axis=1)
        o_ref[...] = (base + own).astype(BF16)


def split_factor(count, most):
    return max(g for g in range(1, most + 1) if count % g == 0)


def body(hidden, down_weight, delta_values, block_ids, variant_slot, row_variant):
    peers = lax.axis_size("cols")
    me = lax.axis_index("cols")
    row_dev, width_f = hidden.shape
    width_d = down_weight.shape[1]
    local_var, count, block_size, _ = delta_values.shape
    variants = variant_slot.shape[0]
    all_rows = row_dev * peers
    capacity = 2 * all_rows // variants
    d_blocks = width_d // block_size
    f_blocks = width_f // block_size
    local_slots = local_var * capacity
    plan = windows(width_f, peers)
    share, window, _, _ = plan
    half = peers // 2
    slice_d = width_d // peers

    scal = jnp.stack([own_shift(plan), me % 2]).astype(jnp.int32)
    smem = pl.BlockSpec(memory_space=pltpu.SMEM)
    vmem = pl.BlockSpec(memory_space=pltpu.VMEM)

    outgoing = pl.pallas_call(
        functools.partial(split_kernel, plan),
        out_shape=jax.ShapeDtypeStruct((peers, row_dev, window), BF16),
        compiler_params=params(),
        name="split_rows",
    )(hidden, row_variant)
    x = lax.all_to_all(outgoing, "cols", 0, 0)

    slots, place = pl.pallas_call(
        functools.partial(route_kernel, plan, capacity),
        out_shape=(
            jax.ShapeDtypeStruct((peers, local_slots, window), BF16),
            jax.ShapeDtypeStruct((all_rows, 1), jnp.int32),
        ),
        in_specs=[smem, vmem, vmem],
        compiler_params=params(),
        name="route",
    )(scal, x, variant_slot.reshape(1, variants))
    arrived = lax.all_to_all(slots, "cols", 0, 0)
    x, place = lax.optimization_barrier((x, place))

    tile = min(512, width_d)
    keep, send = pl.pallas_call(
        functools.partial(base_kernel, plan),
        grid=(width_d // tile,),
        out_shape=(
            jax.ShapeDtypeStruct((half, row_dev, width_d), F32),
            jax.ShapeDtypeStruct((half, row_dev, width_d), BF16),
        ),
        in_specs=[
            smem,
            pl.BlockSpec((peers, row_dev, window), lambda t: (0, 0, 0)),
            pl.BlockSpec((share, tile), lambda t: (0, t)),
        ],
        out_specs=(
            pl.BlockSpec((half, row_dev, tile), lambda t: (0, 0, t)),
            pl.BlockSpec((half, row_dev, tile), lambda t: (0, 0, t)),
        ),
        scratch_shapes=[pltpu.VMEM((all_rows, share), BF16)],
        compiler_params=params(),
        cost_estimate=pl.CostEstimate(
            flops=2 * all_rows * share * width_d,
            bytes_accessed=2 * share * width_d + 6 * all_rows // 2 * width_d,
            transcendentals=0,
        ),
        name="base",
    )(scal, x, down_weight)
    send, arrived = lax.optimization_barrier((send, arrived))
    step = 1
    while True:
        got = lax.ppermute(send, "cols", [(i, i ^ step) for i in range(peers)])
        step *= 2
        if step == peers:
            break
        bit = ((me // step) % 2).astype(jnp.int32).reshape(1)
        left = (keep.shape[0] // 2, row_dev, width_d)
        keep, send = pl.pallas_call(
            halve_kernel,
            in_specs=[smem, vmem, vmem],
            out_shape=(jax.ShapeDtypeStruct(left, F32), jax.ShapeDtypeStruct(left, BF16)),
            compiler_params=params(),
            name="halve",
        )(bit, keep, got)

    group = split_factor(count, 64)
    aligned = slice_d % LANES == 0
    shape = (peers, local_slots, slice_d) if aligned else (local_slots, width_d)
    chunks = local_var * (count // group)
    deltas = pl.pallas_call(
        functools.partial(delta_kernel, plan, d_blocks, group),
        in_specs=[smem, vmem, pl.BlockSpec(memory_space=pl.ANY)],
        out_specs=vmem,
        scratch_shapes=[
            pltpu.VMEM((local_var, f_blocks, capacity, block_size), F32),
            pltpu.VMEM((local_var, d_blocks, capacity, block_size), F32),
            pltpu.VMEM((chunks, group, block_size, block_size), BF16),
            pltpu.SemaphoreType.DMA((chunks,)),
        ],
        out_shape=jax.ShapeDtypeStruct(shape, BF16),
        compiler_params=params(36),
        cost_estimate=pl.CostEstimate(
            flops=2 * local_slots * count * block_size * block_size,
            bytes_accessed=2 * local_var * count * block_size * block_size,
            transcendentals=0,
        ),
        name="delta",
    )(block_ids, arrived, delta_values)
    if not aligned:
        deltas = deltas.reshape(local_slots, peers, slice_d).transpose(1, 0, 2)
    columns = lax.all_to_all(deltas, "cols", 0, 0)
    by_row = pl.pallas_call(
        pick_kernel,
        out_shape=jax.ShapeDtypeStruct((peers, row_dev, slice_d), BF16),
        compiler_params=params(),
        name="pick",
    )(place, columns)
    own = lax.all_to_all(by_row, "cols", 0, 0)
    return pl.pallas_call(
        finish_kernel,
        out_shape=jax.ShapeDtypeStruct((row_dev, width_d), BF16),
        compiler_params=params(),
        name="finish",
    )(keep, got, own)


def solution(mesh):
    return jax.shard_map(
        body,
        mesh=mesh,
        in_specs=(
            P(("groups", "cols"), None),
            P("cols", None),
            P("cols", None, None, None),
            P("cols", None),
            P(),
            P(("groups", "cols"), None),
        ),
        out_specs=P(("groups", "cols"), None),
        check_vma=False,
    )
```

```python
import functools

import jax
import jax.numpy as jnp
from jax import lax
from jax.experimental import pallas as pl
from jax.experimental.pallas import tpu as pltpu
from jax.sharding import PartitionSpec as P

LANES = 128
BF16 = jnp.bfloat16
F32 = jnp.float32


def windows(width_f, peers):
    share = width_f // peers
    most = max((s * share) % LANES for s in range(peers))
    window = -(-(share + most) // LANES) * LANES
    if window == share:
        window += LANES
    last = (width_f - window) // LANES
    starts = [min(s * share // LANES, last) for s in range(peers)]
    return share, window, last, starts


def params(mib=16):
    return pltpu.CompilerParams(vmem_limit_bytes=mib * 1024 * 1024)


def lane_iota(rows, lanes):
    return lax.broadcasted_iota(jnp.int32, (rows, lanes), 1)


def split_kernel(plan, h_ref, id_ref, slot_ref, o_ref):
    share, window, _, starts = plan
    rows = h_ref.shape[0]
    variants = slot_ref.shape[1]
    lane = lane_iota(rows, window)
    diagonal = lax.broadcasted_iota(jnp.int32, (rows, rows), 0) == lane_iota(rows, rows)
    ids = jnp.sum(jnp.where(diagonal, id_ref[...].astype(F32), 0.0), axis=1, keepdims=True)
    named = ids.astype(jnp.int32) == lane_iota(rows, variants)
    slot = jnp.sum(jnp.where(named, slot_ref[...].astype(F32), 0.0), axis=1, keepdims=True)
    for s, b in enumerate(starts):
        spare = (s * share - b * LANES + share) % window
        piece = h_ref[:, b * LANES : b * LANES + window].astype(F32)
        o_ref[s] = jnp.where(lane == spare, slot, piece).astype(BF16)


def own_shift(plan):
    share, _, last, _ = plan
    start = lax.axis_index("cols") * share
    return start - jnp.minimum(start // LANES, last) * LANES


def route_kernel(plan, capacity, shift_ref, x_ref, o_ref, place_ref):
    share, window, _, _ = plan
    peers, row_dev, _ = x_ref.shape
    rows = peers * row_dev
    slots = o_ref.shape[0] * o_ref.shape[1]
    variants = slots // capacity
    shift = shift_ref[0]
    x = x_ref[...].reshape(rows, window).astype(F32)
    lane = lane_iota(rows, window)
    spare = lax.rem(shift + share, window)
    slot = jnp.sum(jnp.where(lane == spare, x, 0.0), axis=1, keepdims=True)
    data = jnp.where((lane >= shift) & (lane < shift + share), x, 0.0).astype(BF16)
    onehot = jnp.where(slot.astype(jnp.int32) == lane_iota(rows, variants), 1.0, 0.0)
    row_i = lax.broadcasted_iota(jnp.int32, (rows, rows), 0)
    row_j = lane_iota(rows, rows)
    earlier = jnp.where(row_j < row_i, 1.0, 0.0).astype(BF16)
    before = jnp.dot(earlier, onehot.astype(BF16), preferred_element_type=F32)
    rank = jnp.sum(before * onehot, axis=1, keepdims=True)
    place = slot * capacity + rank
    place_ref[...] = place.astype(jnp.int32)
    across = jnp.sum(jnp.where(row_i == row_j, place, 0.0), axis=0, keepdims=True)
    pick = across.astype(jnp.int32) == lax.broadcasted_iota(jnp.int32, (slots, rows), 0)
    pick = jnp.where(pick, 1.0, 0.0).astype(BF16)
    filled = jnp.dot(pick, data, preferred_element_type=F32).astype(BF16)
    o_ref[...] = filled.reshape(o_ref.shape)


def base_kernel(plan, scal_ref, x_ref, w_ref, place_ref, o_ref, own_ref, mine_ref):
    share, window, _, _ = plan
    peers, row_dev, _ = x_ref.shape

    @pl.when(pl.program_id(0) == 0)
    def _():
        bit = scal_ref[1]
        for side in (0, 1):
            which = bit if side == 0 else 1 - bit
            for q in range(peers // 2):
                piece = x_ref[2 * q + which].astype(F32)
                piece = pltpu.roll(piece, window - scal_ref[0], 1)
                at = (side * (peers // 2) + q) * row_dev
                mine_ref[at : at + row_dev] = piece[:, :share].astype(BF16)
                own_ref[at : at + row_dev] = place_ref[2 * q + which]

    o_ref[...] = jnp.dot(mine_ref[...], w_ref[...], preferred_element_type=F32)


def delta_kernel(
    plan, d_blocks, group, scal_ref, ids_ref, x_hbm, v_hbm, base_hbm, own_ref, *rest
):
    keeps, sends = rest[0:2], rest[2:4]
    rows_ref, acc_ref, held_ref, x_ref, base_ref, sems, x_sem, base_sem = rest[4:]
    _, window, _, starts = plan
    local_var, f_blocks, capacity, _ = rows_ref.shape
    chunks, _, size, _ = held_ref.shape
    per = chunks // local_var

    def fetch(c):
        source = v_hbm.at[c // per, pl.ds((c % per) * group, group)]
        return pltpu.make_async_copy(source, held_ref.at[c], sems.at[c])

    x_copy = pltpu.make_async_copy(x_hbm, x_ref, x_sem)
    x_copy.start()
    for c in range(chunks):
        fetch(c).start()
    base_copy = pltpu.make_async_copy(base_hbm, base_ref, base_sem)
    base_copy.start()

    acc_ref[...] = jnp.zeros_like(acc_ref)
    x_copy.wait()
    done = set()
    for s, b in enumerate(starts):
        for k in range(window // LANES):
            tile = x_ref[s, :, k * LANES : (k + 1) * LANES].astype(F32)
            for v in range(local_var):
                part = tile[v * capacity : (v + 1) * capacity]
                if b + k in done:
                    part = part + rows_ref[v, b + k]
                rows_ref[v, b + k] = part
            done.add(b + k)

    zeros = jnp.zeros((capacity, size), F32)

    def one_chunk(c, carry):
        var = lax.div(c, per)
        first = lax.rem(c, per) * group
        pltpu.make_async_copy(
            v_hbm.at[var, pl.ds(first, group)], held_ref.at[c], sems.at[c]
        ).wait()
        sums = []
        for n in range(0, group, 2):
            blocks = [ids_ref[var, first + m] for m in range(n, min(n + 2, group))]
            lhs = [rows_ref[var, lax.div(block, d_blocks)] for block in blocks]
            if len(blocks) == 2:
                upper = jnp.concatenate([lhs[0], zeros], axis=1)
                lower = jnp.concatenate([zeros, lhs[1]], axis=1)
                left = jnp.concatenate([upper, lower], axis=0).astype(BF16)
                right = held_ref[c, n : n + 2].reshape(2 * size, size)
            else:
                left = lhs[0].astype(BF16)
                right = held_ref[c, n]
            product = jnp.dot(left, right, preferred_element_type=F32)
            for q, block in enumerate(blocks):
                part = product[q * capacity : (q + 1) * capacity]
                sums.append((lax.rem(block, d_blocks), part))
        for column, part in sums:
            acc_ref[var, column] += part
        return carry

    lax.fori_loop(0, chunks, one_chunk, 0)

    all_rows = base_ref.shape[0]
    slots = local_var * capacity
    join = own_ref[...] - scal_ref[2] == lane_iota(all_rows, slots)
    join = jnp.where(join, 1.0, 0.0).astype(BF16)
    per_side = d_blocks // 2
    base_copy.wait()
    for j in range(d_blocks):
        whole = jnp.concatenate([acc_ref[v, j] for v in range(local_var)], axis=0).astype(BF16)
        total = base_ref[:, j * size : (j + 1) * size]
        total = total + jnp.dot(join, whole, preferred_element_type=F32)
        keep_ref, send_ref = keeps[j // per_side], sends[j // per_side]
        at = slice((j % per_side) * size, (j % per_side + 1) * size)
        tile = keep_ref.shape[:2] + (size,)
        keep_ref[:, :, at] = total[: all_rows // 2].reshape(tile)
        send_ref[:, :, at] = total[all_rows // 2 :].astype(BF16).reshape(tile)


def halve_kernel(stride, bit_ref, keep_ref, got_ref, next_ref, send_ref):
    bit = bit_ref[0]
    for q in range(next_ref.shape[0]):
        first = q // stride * 2 * stride + q % stride
        mine, other = first + stride * bit, first + stride * (1 - bit)
        next_ref[q] = keep_ref[mine] + got_ref[mine].astype(F32)
        send_ref[q] = (keep_ref[other] + got_ref[other].astype(F32)).astype(BF16)


def finish_kernel(*refs):
    o_ref = refs[-1]
    cols = o_ref.shape[1] // 2
    for side in (0, 1):
        keep_ref, got_ref = refs[2 * side : 2 * side + 2]
        total = keep_ref[0] + got_ref[0].astype(F32)
        o_ref[:, side * cols : (side + 1) * cols] = total.astype(BF16)


def split_factor(count, most):
    return max(g for g in range(1, most + 1) if count % g == 0)


def body(hidden, down_weight, delta_values, block_ids, variant_slot, row_variant):
    peers = lax.axis_size("cols")
    me = lax.axis_index("cols")
    row_dev, width_f = hidden.shape
    width_d = down_weight.shape[1]
    local_var, count, block_size, _ = delta_values.shape
    variants = variant_slot.shape[0]
    all_rows = row_dev * peers
    capacity = 2 * all_rows // variants
    d_blocks = width_d // block_size
    f_blocks = width_f // block_size
    local_slots = local_var * capacity
    plan = windows(width_f, peers)
    share, window, _, _ = plan
    half = peers // 2

    scal = jnp.stack([own_shift(plan), me % 2, me * local_slots]).astype(jnp.int32)
    smem = pl.BlockSpec(memory_space=pltpu.SMEM)
    vmem = pl.BlockSpec(memory_space=pltpu.VMEM)
    anywhere = pl.BlockSpec(memory_space=pl.ANY)

    outgoing = pl.pallas_call(
        functools.partial(split_kernel, plan),
        out_shape=jax.ShapeDtypeStruct((peers, row_dev, window), BF16),
        compiler_params=params(),
        name="split_rows",
    )(hidden, row_variant.reshape(1, row_dev), variant_slot.reshape(1, variants))
    x = lax.all_to_all(outgoing, "cols", 0, 0)

    slots, place = pl.pallas_call(
        functools.partial(route_kernel, plan, capacity),
        out_shape=(
            jax.ShapeDtypeStruct((peers, local_slots, window), BF16),
            jax.ShapeDtypeStruct((all_rows, 1), jnp.int32),
        ),
        in_specs=[smem, vmem],
        compiler_params=params(),
        name="route",
    )(scal, x)
    arrived = lax.all_to_all(slots, "cols", 0, 0)

    tile = min(512, width_d)
    base, own = pl.pallas_call(
        functools.partial(base_kernel, plan),
        grid=(width_d // tile,),
        out_shape=(
            jax.ShapeDtypeStruct((all_rows, width_d), F32),
            jax.ShapeDtypeStruct((all_rows, 1), jnp.int32),
        ),
        in_specs=[
            smem,
            pl.BlockSpec((peers, row_dev, window), lambda t: (0, 0, 0)),
            pl.BlockSpec((share, tile), lambda t: (0, t)),
            pl.BlockSpec((peers, row_dev, 1), lambda t: (0, 0, 0)),
        ],
        out_specs=(
            pl.BlockSpec((all_rows, tile), lambda t: (0, t)),
            pl.BlockSpec((all_rows, 1), lambda t: (0, 0)),
        ),
        scratch_shapes=[pltpu.VMEM((all_rows, share), BF16)],
        compiler_params=params(60),
        cost_estimate=pl.CostEstimate(
            flops=2 * all_rows * share * width_d,
            bytes_accessed=2 * share * width_d + 4 * all_rows * width_d,
            transcendentals=0,
        ),
        name="base",
    )(scal, x, down_weight, place.reshape(peers, row_dev, 1))

    group = split_factor(count, 64)
    chunks = local_var * (count // group)
    part = (half, row_dev, width_d // 2)
    joined = pl.pallas_call(
        functools.partial(delta_kernel, plan, d_blocks, group),
        in_specs=[smem, smem, anywhere, anywhere, anywhere, vmem],
        out_specs=[vmem] * 4,
        scratch_shapes=[
            pltpu.VMEM((local_var, f_blocks, capacity, block_size), F32),
            pltpu.VMEM((local_var, d_blocks, capacity, block_size), F32),
            pltpu.VMEM((chunks, group, block_size, block_size), BF16),
            pltpu.VMEM((peers, local_slots, window), BF16),
            pltpu.VMEM((all_rows, width_d), F32),
            pltpu.SemaphoreType.DMA((chunks,)),
            pltpu.SemaphoreType.DMA,
            pltpu.SemaphoreType.DMA,
        ],
        out_shape=[jax.ShapeDtypeStruct(part, F32)] * 2 + [jax.ShapeDtypeStruct(part, BF16)] * 2,
        compiler_params=params(60),
        cost_estimate=pl.CostEstimate(
            flops=2 * local_slots * count * block_size * block_size,
            bytes_accessed=2 * local_var * count * block_size * block_size,
            transcendentals=0,
        ),
        name="delta",
    )(scal, block_ids, arrived, delta_values, base, own)

    above = [1 << k for k in range(1, peers.bit_length() - 1)]
    ends = []
    for side, order in enumerate((above, above[1:] + above[:1])):
        keep, send = joined[side], joined[2 + side]
        open_bits = list(above)
        got = lax.ppermute(send, "cols", [(i, i ^ 1) for i in range(peers)])
        for step in order:
            stride = 1 << open_bits.index(step)
            open_bits.remove(step)
            bit = ((me // step) % 2).astype(jnp.int32).reshape(1)
            left = (keep.shape[0] // 2,) + part[1:]
            keep, send = pl.pallas_call(
                functools.partial(halve_kernel, stride),
                in_specs=[smem, vmem, vmem],
                out_shape=(jax.ShapeDtypeStruct(left, F32), jax.ShapeDtypeStruct(left, BF16)),
                compiler_params=params(),
                name="halve",
            )(bit, keep, got)
            got = lax.ppermute(send, "cols", [(i, i ^ step) for i in range(peers)])
        ends += [keep, got]
    return pl.pallas_call(
        finish_kernel,
        out_shape=jax.ShapeDtypeStruct((row_dev, width_d), BF16),
        compiler_params=params(),
        name="finish",
    )(*ends)


def solution(mesh):
    return jax.shard_map(
        body,
        mesh=mesh,
        in_specs=(
            P(("groups", "cols"), None),
            P("cols", None),
            P("cols", None, None, None),
            P("cols", None),
            P(),
            P(("groups", "cols"), None),
        ),
        out_specs=P(("groups", "cols"), None),
        check_vma=False,
    )
```

```python
import functools

import jax
import jax.numpy as jnp
from jax import lax
from jax.experimental import pallas as pl
from jax.experimental.pallas import tpu as pltpu
from jax.sharding import PartitionSpec as P

LANES = 128
BF16 = jnp.bfloat16
F32 = jnp.float32


def windows(width_f, peers):
    share = width_f // peers
    most = max((s * share) % LANES for s in range(peers))
    window = -(-(share + most) // LANES) * LANES
    if window == share:
        window += LANES
    last = (width_f - window) // LANES
    starts = [min(s * share // LANES, last) for s in range(peers)]
    return share, window, last, starts


def params(mib=16):
    return pltpu.CompilerParams(vmem_limit_bytes=mib * 1024 * 1024)


def lane_iota(rows, lanes):
    return lax.broadcasted_iota(jnp.int32, (rows, lanes), 1)


def split_kernel(plan, h_ref, id_ref, slot_ref, o_ref):
    share, window, _, starts = plan
    rows = h_ref.shape[0]
    variants = slot_ref.shape[1]
    lane = lane_iota(rows, window)
    diagonal = lax.broadcasted_iota(jnp.int32, (rows, rows), 0) == lane_iota(rows, rows)
    ids = jnp.sum(jnp.where(diagonal, id_ref[...].astype(F32), 0.0), axis=1, keepdims=True)
    named = ids.astype(jnp.int32) == lane_iota(rows, variants)
    slot = jnp.sum(jnp.where(named, slot_ref[...].astype(F32), 0.0), axis=1, keepdims=True)
    for s, b in enumerate(starts):
        spare = (s * share - b * LANES + share) % window
        piece = h_ref[:, b * LANES : b * LANES + window].astype(F32)
        o_ref[s] = jnp.where(lane == spare, slot, piece).astype(BF16)


def own_shift(plan):
    share, _, last, _ = plan
    start = lax.axis_index("cols") * share
    return start - jnp.minimum(start // LANES, last) * LANES


def route_kernel(plan, capacity, shift_ref, x_ref, o_ref, place_ref):
    share, window, _, _ = plan
    peers, row_dev, _ = x_ref.shape
    rows = peers * row_dev
    slots = o_ref.shape[0] * o_ref.shape[1]
    variants = slots // capacity
    shift = shift_ref[0]
    x = x_ref[...].reshape(rows, window).astype(F32)
    lane = lane_iota(rows, window)
    spare = lax.rem(shift + share, window)
    slot = jnp.sum(jnp.where(lane == spare, x, 0.0), axis=1, keepdims=True)
    data = jnp.where((lane >= shift) & (lane < shift + share), x, 0.0).astype(BF16)
    onehot = jnp.where(slot.astype(jnp.int32) == lane_iota(rows, variants), 1.0, 0.0)
    row_i = lax.broadcasted_iota(jnp.int32, (rows, rows), 0)
    row_j = lane_iota(rows, rows)
    earlier = jnp.where(row_j < row_i, 1.0, 0.0).astype(BF16)
    before = jnp.dot(earlier, onehot.astype(BF16), preferred_element_type=F32)
    rank = jnp.sum(before * onehot, axis=1, keepdims=True)
    place = slot * capacity + rank
    place_ref[...] = place.astype(jnp.int32)
    across = jnp.sum(jnp.where(row_i == row_j, place, 0.0), axis=0, keepdims=True)
    pick = across.astype(jnp.int32) == lax.broadcasted_iota(jnp.int32, (slots, rows), 0)
    pick = jnp.where(pick, 1.0, 0.0).astype(BF16)
    filled = jnp.dot(pick, data, preferred_element_type=F32).astype(BF16)
    o_ref[...] = filled.reshape(o_ref.shape)


def base_kernel(plan, scal_ref, x_ref, w_ref, keep_ref, send_ref, mine_ref):
    share, window, _, _ = plan
    peers, row_dev, _ = x_ref.shape
    half = peers // 2 * row_dev

    @pl.when(pl.program_id(0) == 0)
    def _():
        bit = scal_ref[1]
        for side in (0, 1):
            which = bit if side == 0 else 1 - bit
            for q in range(peers // 2):
                piece = x_ref[2 * q + which].astype(F32)
                piece = pltpu.roll(piece, window - scal_ref[0], 1)
                at = side * half + q * row_dev
                mine_ref[at : at + row_dev] = piece[:, :share].astype(BF16)

    both = jnp.dot(mine_ref[...], w_ref[...], preferred_element_type=F32)
    keep_ref[...] = both[:half].reshape(keep_ref.shape)
    send_ref[...] = both[half:].astype(BF16).reshape(send_ref.shape)


def delta_kernel(plan, d_blocks, group, ids_ref, x_ref, v_hbm, o_ref, rows_ref, acc_ref, held_ref, sems):
    _, window, _, starts = plan
    local_var, f_blocks, capacity, _ = rows_ref.shape
    chunks, _, size, _ = held_ref.shape
    per = chunks // local_var

    def fetch(c):
        source = v_hbm.at[c // per, pl.ds((c % per) * group, group)]
        return pltpu.make_async_copy(source, held_ref.at[c], sems.at[c])

    for c in range(chunks):
        fetch(c).start()

    acc_ref[...] = jnp.zeros_like(acc_ref)
    done = set()
    for s, b in enumerate(starts):
        for k in range(window // LANES):
            tile = x_ref[s, :, k * LANES : (k + 1) * LANES].astype(F32)
            for v in range(local_var):
                part = tile[v * capacity : (v + 1) * capacity]
                if b + k in done:
                    part = part + rows_ref[v, b + k]
                rows_ref[v, b + k] = part
            done.add(b + k)

    zeros = jnp.zeros((capacity, size), F32)

    def one_chunk(c, carry):
        var = lax.div(c, per)
        first = lax.rem(c, per) * group
        pltpu.make_async_copy(
            v_hbm.at[var, pl.ds(first, group)], held_ref.at[c], sems.at[c]
        ).wait()
        sums = []
        for n in range(0, group, 2):
            blocks = [ids_ref[var, first + m] for m in range(n, min(n + 2, group))]
            lhs = [rows_ref[var, lax.div(block, d_blocks)] for block in blocks]
            if len(blocks) == 2:
                upper = jnp.concatenate([lhs[0], zeros], axis=1)
                lower = jnp.concatenate([zeros, lhs[1]], axis=1)
                left = jnp.concatenate([upper, lower], axis=0).astype(BF16)
                right = held_ref[c, n : n + 2].reshape(2 * size, size)
            else:
                left = lhs[0].astype(BF16)
                right = held_ref[c, n]
            product = jnp.dot(left, right, preferred_element_type=F32)
            for q, block in enumerate(blocks):
                part = product[q * capacity : (q + 1) * capacity]
                sums.append((lax.rem(block, d_blocks), part))
        for column, part in sums:
            acc_ref[var, column] += part
        return carry

    lax.fori_loop(0, chunks, one_chunk, 0)
    for j in range(d_blocks):
        whole = jnp.concatenate([acc_ref[v, j] for v in range(local_var)], axis=0)
        if len(o_ref.shape) == 3:
            per_peer = o_ref.shape[2] // LANES
            k = j % per_peer
            o_ref[j // per_peer, :, k * LANES : (k + 1) * LANES] = whole.astype(BF16)
        else:
            o_ref[:, j * LANES : (j + 1) * LANES] = whole.astype(BF16)


def pick_kernel(place_ref, c_ref, o_ref):
    peers, per_owner, cols = c_ref.shape
    slots = peers * per_owner
    rows = place_ref.shape[0]
    pick = place_ref[...] == lane_iota(rows, slots)
    pick = jnp.where(pick, 1.0, 0.0).astype(BF16)
    found = jnp.dot(pick, c_ref[...].reshape(slots, cols), preferred_element_type=F32)
    o_ref[...] = found.astype(BF16).reshape(o_ref.shape)


def halve_kernel(bit_ref, keep_ref, got_ref, next_ref, send_ref):
    bit = bit_ref[0]
    for q in range(next_ref.shape[0]):
        mine, other = 2 * q + bit, 2 * q + 1 - bit
        next_ref[q] = keep_ref[mine] + got_ref[mine].astype(F32)
        send_ref[q] = (keep_ref[other] + got_ref[other].astype(F32)).astype(BF16)


def finish_kernel(keep_ref, got_ref, own_ref, o_ref):
    peers, _, cols = own_ref.shape
    base = keep_ref[0] + got_ref[0].astype(F32)
    if cols % LANES == 0:
        for s in range(peers):
            at = slice(s * cols, (s + 1) * cols)
            o_ref[:, at] = (base[:, at] + own_ref[s].astype(F32)).astype(BF16)
    else:
        own = jnp.concatenate([own_ref[s].astype(F32) for s in range(peers)], axis=1)
        o_ref[...] = (base + own).astype(BF16)


def split_factor(count, most):
    return max(g for g in range(1, most + 1) if count % g == 0)


def body(hidden, down_weight, delta_values, block_ids, variant_slot, row_variant):
    peers = lax.axis_size("cols")
    me = lax.axis_index("cols")
    row_dev, width_f = hidden.shape
    width_d = down_weight.shape[1]
    local_var, count, block_size, _ = delta_values.shape
    variants = variant_slot.shape[0]
    all_rows = row_dev * peers
    capacity = 2 * all_rows // variants
    d_blocks = width_d // block_size
    f_blocks = width_f // block_size
    local_slots = local_var * capacity
    plan = windows(width_f, peers)
    share, window, _, _ = plan
    half = peers // 2
    slice_d = width_d // peers

    scal = jnp.stack([own_shift(plan), me % 2]).astype(jnp.int32)
    smem = pl.BlockSpec(memory_space=pltpu.SMEM)
    vmem = pl.BlockSpec(memory_space=pltpu.VMEM)

    outgoing = pl.pallas_call(
        functools.partial(split_kernel, plan),
        out_shape=jax.ShapeDtypeStruct((peers, row_dev, window), BF16),
        compiler_params=params(),
        name="split_rows",
    )(hidden, row_variant.reshape(1, row_dev), variant_slot.reshape(1, variants))
    x = lax.all_to_all(outgoing, "cols", 0, 0)

    slots, place = pl.pallas_call(
        functools.partial(route_kernel, plan, capacity),
        out_shape=(
            jax.ShapeDtypeStruct((peers, local_slots, window), BF16),
            jax.ShapeDtypeStruct((all_rows, 1), jnp.int32),
        ),
        in_specs=[smem, vmem],
        compiler_params=params(),
        name="route",
    )(scal, x)
    arrived = lax.all_to_all(slots, "cols", 0, 0)
    x, place = lax.optimization_barrier((x, place))

    tile = min(512, width_d)
    keep, send = pl.pallas_call(
        functools.partial(base_kernel, plan),
        grid=(width_d // tile,),
        out_shape=(
            jax.ShapeDtypeStruct((half, row_dev, width_d), F32),
            jax.ShapeDtypeStruct((half, row_dev, width_d), BF16),
        ),
        in_specs=[
            smem,
            pl.BlockSpec((peers, row_dev, window), lambda t: (0, 0, 0)),
            pl.BlockSpec((share, tile), lambda t: (0, t)),
        ],
        out_specs=(
            pl.BlockSpec((half, row_dev, tile), lambda t: (0, 0, t)),
            pl.BlockSpec((half, row_dev, tile), lambda t: (0, 0, t)),
        ),
        scratch_shapes=[pltpu.VMEM((all_rows, share), BF16)],
        compiler_params=params(),
        cost_estimate=pl.CostEstimate(
            flops=2 * all_rows * share * width_d,
            bytes_accessed=2 * share * width_d + 6 * all_rows // 2 * width_d,
            transcendentals=0,
        ),
        name="base",
    )(scal, x, down_weight)
    step = 1
    while True:
        got = lax.ppermute(send, "cols", [(i, i ^ step) for i in range(peers)])
        step *= 2
        if step == peers:
            break
        bit = ((me // step) % 2).astype(jnp.int32).reshape(1)
        left = (keep.shape[0] // 2, row_dev, width_d)
        keep, send = pl.pallas_call(
            halve_kernel,
            in_specs=[smem, vmem, vmem],
            out_shape=(jax.ShapeDtypeStruct(left, F32), jax.ShapeDtypeStruct(left, BF16)),
            compiler_params=params(),
            name="halve",
        )(bit, keep, got)
        if step == 2:
            send, arrived = lax.optimization_barrier((send, arrived))

    group = split_factor(count, 64)
    aligned = slice_d % LANES == 0
    shape = (peers, local_slots, slice_d) if aligned else (local_slots, width_d)
    chunks = local_var * (count // group)
    deltas = pl.pallas_call(
        functools.partial(delta_kernel, plan, d_blocks, group),
        in_specs=[smem, vmem, pl.BlockSpec(memory_space=pl.ANY)],
        out_specs=vmem,
        scratch_shapes=[
            pltpu.VMEM((local_var, f_blocks, capacity, block_size), F32),
            pltpu.VMEM((local_var, d_blocks, capacity, block_size), F32),
            pltpu.VMEM((chunks, group, block_size, block_size), BF16),
            pltpu.SemaphoreType.DMA((chunks,)),
        ],
        out_shape=jax.ShapeDtypeStruct(shape, BF16),
        compiler_params=params(36),
        cost_estimate=pl.CostEstimate(
            flops=2 * local_slots * count * block_size * block_size,
            bytes_accessed=2 * local_var * count * block_size * block_size,
            transcendentals=0,
        ),
        name="delta",
    )(block_ids, arrived, delta_values)
    if not aligned:
        deltas = deltas.reshape(local_slots, peers, slice_d).transpose(1, 0, 2)
    columns = lax.all_to_all(deltas, "cols", 0, 0)
    by_row = pl.pallas_call(
        pick_kernel,
        out_shape=jax.ShapeDtypeStruct((peers, row_dev, slice_d), BF16),
        compiler_params=params(),
        name="pick",
    )(place, columns)
    own = lax.all_to_all(by_row, "cols", 0, 0)
    return pl.pallas_call(
        finish_kernel,
        out_shape=jax.ShapeDtypeStruct((row_dev, width_d), BF16),
        compiler_params=params(),
        name="finish",
    )(keep, got, own)


def solution(mesh):
    return jax.shard_map(
        body,
        mesh=mesh,
        in_specs=(
            P(("groups", "cols"), None),
            P("cols", None),
            P("cols", None, None, None),
            P("cols", None),
            P(),
            P(("groups", "cols"), None),
        ),
        out_specs=P(("groups", "cols"), None),
        check_vma=False,
    )
```

```python
import functools

import jax
import jax.numpy as jnp
from jax import lax
from jax.experimental import pallas as pl
from jax.experimental.pallas import tpu as pltpu
from jax.sharding import PartitionSpec as P

LANES = 128
BF16 = jnp.bfloat16
F32 = jnp.float32


def windows(width_f, peers):
    share = width_f // peers
    most = max((s * share) % LANES for s in range(peers))
    window = -(-(share + most) // LANES) * LANES
    if window == share:
        window += LANES
    last = (width_f - window) // LANES
    starts = [min(s * share // LANES, last) for s in range(peers)]
    return share, window, last, starts


def params(mib=16):
    return pltpu.CompilerParams(vmem_limit_bytes=mib * 1024 * 1024)


def lane_iota(rows, lanes):
    return lax.broadcasted_iota(jnp.int32, (rows, lanes), 1)


def split_kernel(plan, h_hbm, id_hbm, slot_hbm, o_ref, h_ref, id_ref, slot_ref, sems):
    share, window, _, starts = plan
    rows, width = h_ref.shape
    variants = slot_ref.shape[1]
    cut = width // LANES // 2 * LANES
    halves = (slice(0, cut), slice(cut, width))
    copies = [
        pltpu.make_async_copy(id_hbm, id_ref, sems.at[0]),
        pltpu.make_async_copy(slot_hbm, slot_ref, sems.at[1]),
        pltpu.make_async_copy(h_hbm.at[:, halves[0]], h_ref.at[:, halves[0]], sems.at[2]),
        pltpu.make_async_copy(h_hbm.at[:, halves[1]], h_ref.at[:, halves[1]], sems.at[3]),
    ]
    for copy in copies:
        copy.start()
    copies[0].wait()
    copies[1].wait()
    lane = lane_iota(rows, window)
    diagonal = lax.broadcasted_iota(jnp.int32, (rows, rows), 0) == lane_iota(rows, rows)
    ids = jnp.sum(jnp.where(diagonal, id_ref[...].astype(F32), 0.0), axis=1, keepdims=True)
    named = ids.astype(jnp.int32) == lane_iota(rows, variants)
    slot = jnp.sum(jnp.where(named, slot_ref[...].astype(F32), 0.0), axis=1, keepdims=True)
    copies[2].wait()
    late = True
    for s, b in enumerate(starts):
        if late and b * LANES + window > cut:
            copies[3].wait()
            late = False
        spare = (s * share - b * LANES + share) % window
        piece = h_ref[:, b * LANES : b * LANES + window].astype(F32)
        o_ref[s] = jnp.where(lane == spare, slot, piece).astype(BF16)


def own_shift(plan):
    share, _, last, _ = plan
    start = lax.axis_index("cols") * share
    return start - jnp.minimum(start // LANES, last) * LANES


def route_kernel(plan, capacity, shift_ref, x_ref, o_ref, place_ref):
    share, window, _, _ = plan
    peers, row_dev, _ = x_ref.shape
    rows = peers * row_dev
    slots = o_ref.shape[0] * o_ref.shape[1]
    variants = slots // capacity
    shift = shift_ref[0]
    x = x_ref[...].reshape(rows, window).astype(F32)
    lane = lane_iota(rows, window)
    spare = lax.rem(shift + share, window)
    slot = jnp.sum(jnp.where(lane == spare, x, 0.0), axis=1, keepdims=True)
    data = jnp.where((lane >= shift) & (lane < shift + share), x, 0.0).astype(BF16)
    onehot = jnp.where(slot.astype(jnp.int32) == lane_iota(rows, variants), 1.0, 0.0)
    row_i = lax.broadcasted_iota(jnp.int32, (rows, rows), 0)
    row_j = lane_iota(rows, rows)
    earlier = jnp.where(row_j < row_i, 1.0, 0.0).astype(BF16)
    before = jnp.dot(earlier, onehot.astype(BF16), preferred_element_type=F32)
    rank = jnp.sum(before * onehot, axis=1, keepdims=True)
    place = slot * capacity + rank
    place_ref[...] = place.astype(jnp.int32)
    across = jnp.sum(jnp.where(row_i == row_j, place, 0.0), axis=0, keepdims=True)
    pick = across.astype(jnp.int32) == lax.broadcasted_iota(jnp.int32, (slots, rows), 0)
    pick = jnp.where(pick, 1.0, 0.0).astype(BF16)
    filled = jnp.dot(pick, data, preferred_element_type=F32).astype(BF16)
    o_ref[...] = filled.reshape(o_ref.shape)


def base_kernel(plan, scal_ref, x_ref, w_ref, keep_ref, send_ref, mine_ref):
    share, window, _, _ = plan
    peers, row_dev, _ = x_ref.shape
    half = peers // 2 * row_dev

    @pl.when(pl.program_id(0) == 0)
    def _():
        bit = scal_ref[1]
        for side in (0, 1):
            which = bit if side == 0 else 1 - bit
            for q in range(peers // 2):
                piece = x_ref[2 * q + which].astype(F32)
                piece = pltpu.roll(piece, window - scal_ref[0], 1)
                at = side * half + q * row_dev
                mine_ref[at : at + row_dev] = piece[:, :share].astype(BF16)

    both = jnp.dot(mine_ref[...], w_ref[...], preferred_element_type=F32)
    keep_ref[...] = both[:half].reshape(keep_ref.shape)
    send_ref[...] = both[half:].astype(BF16).reshape(send_ref.shape)


def delta_kernel(plan, d_blocks, group, ids_ref, x_ref, v_hbm, o_ref, rows_ref, acc_ref, held_ref, sems):
    _, window, _, starts = plan
    local_var, f_blocks, capacity, _ = rows_ref.shape
    chunks, _, size, _ = held_ref.shape
    per = chunks // local_var

    def fetch(c):
        source = v_hbm.at[c // per, pl.ds((c % per) * group, group)]
        return pltpu.make_async_copy(source, held_ref.at[c], sems.at[c])

    for c in range(chunks):
        fetch(c).start()

    acc_ref[...] = jnp.zeros_like(acc_ref)
    done = set()
    for s, b in enumerate(starts):
        for k in range(window // LANES):
            tile = x_ref[s, :, k * LANES : (k + 1) * LANES].astype(F32)
            for v in range(local_var):
                part = tile[v * capacity : (v + 1) * capacity]
                if b + k in done:
                    part = part + rows_ref[v, b + k]
                rows_ref[v, b + k] = part
            done.add(b + k)

    zeros = jnp.zeros((capacity, size), F32)

    def one_chunk(c, carry):
        var = lax.div(c, per)
        first = lax.rem(c, per) * group
        pltpu.make_async_copy(
            v_hbm.at[var, pl.ds(first, group)], held_ref.at[c], sems.at[c]
        ).wait()
        sums = []
        for n in range(0, group, 2):
            blocks = [ids_ref[var, first + m] for m in range(n, min(n + 2, group))]
            lhs = [rows_ref[var, lax.div(block, d_blocks)] for block in blocks]
            if len(blocks) == 2:
                upper = jnp.concatenate([lhs[0], zeros], axis=1)
                lower = jnp.concatenate([zeros, lhs[1]], axis=1)
                left = jnp.concatenate([upper, lower], axis=0).astype(BF16)
                right = held_ref[c, n : n + 2].reshape(2 * size, size)
            else:
                left = lhs[0].astype(BF16)
                right = held_ref[c, n]
            product = jnp.dot(left, right, preferred_element_type=F32)
            for q, block in enumerate(blocks):
                part = product[q * capacity : (q + 1) * capacity]
                sums.append((lax.rem(block, d_blocks), part))
        for column, part in sums:
            acc_ref[var, column] += part
        return carry

    lax.fori_loop(0, chunks, one_chunk, 0)
    for j in range(d_blocks):
        whole = jnp.concatenate([acc_ref[v, j] for v in range(local_var)], axis=0)
        if len(o_ref.shape) == 3:
            per_peer = o_ref.shape[2] // LANES
            k = j % per_peer
            o_ref[j // per_peer, :, k * LANES : (k + 1) * LANES] = whole.astype(BF16)
        else:
            o_ref[:, j * LANES : (j + 1) * LANES] = whole.astype(BF16)


def pick_kernel(place_ref, c_ref, o_ref):
    peers, per_owner, cols = c_ref.shape
    slots = peers * per_owner
    rows = place_ref.shape[0]
    pick = place_ref[...] == lane_iota(rows, slots)
    pick = jnp.where(pick, 1.0, 0.0).astype(BF16)
    found = jnp.dot(pick, c_ref[...].reshape(slots, cols), preferred_element_type=F32)
    o_ref[...] = found.astype(BF16).reshape(o_ref.shape)


def halve_kernel(bit_ref, keep_ref, got_ref, next_ref, send_ref):
    bit = bit_ref[0]
    for q in range(next_ref.shape[0]):
        mine, other = 2 * q + bit, 2 * q + 1 - bit
        next_ref[q] = keep_ref[mine] + got_ref[mine].astype(F32)
        send_ref[q] = (keep_ref[other] + got_ref[other].astype(F32)).astype(BF16)


def finish_kernel(keep_ref, got_ref, own_ref, o_ref):
    peers, _, cols = own_ref.shape
    base = keep_ref[0] + got_ref[0].astype(F32)
    if cols % LANES == 0:
        for s in range(peers):
            at = slice(s * cols, (s + 1) * cols)
            o_ref[:, at] = (base[:, at] + own_ref[s].astype(F32)).astype(BF16)
    else:
        own = jnp.concatenate([own_ref[s].astype(F32) for s in range(peers)], axis=1)
        o_ref[...] = (base + own).astype(BF16)


def split_factor(count, most):
    return max(g for g in range(1, most + 1) if count % g == 0)


def body(hidden, down_weight, delta_values, block_ids, variant_slot, row_variant):
    peers = lax.axis_size("cols")
    me = lax.axis_index("cols")
    row_dev, width_f = hidden.shape
    width_d = down_weight.shape[1]
    local_var, count, block_size, _ = delta_values.shape
    variants = variant_slot.shape[0]
    all_rows = row_dev * peers
    capacity = 2 * all_rows // variants
    d_blocks = width_d // block_size
    f_blocks = width_f // block_size
    local_slots = local_var * capacity
    plan = windows(width_f, peers)
    share, window, _, _ = plan
    half = peers // 2
    slice_d = width_d // peers

    scal = jnp.stack([own_shift(plan), me % 2]).astype(jnp.int32)
    smem = pl.BlockSpec(memory_space=pltpu.SMEM)
    vmem = pl.BlockSpec(memory_space=pltpu.VMEM)
    anywhere = pl.BlockSpec(memory_space=pl.ANY)

    outgoing = pl.pallas_call(
        functools.partial(split_kernel, plan),
        in_specs=[anywhere] * 3,
        out_shape=jax.ShapeDtypeStruct((peers, row_dev, window), BF16),
        scratch_shapes=[
            pltpu.VMEM((row_dev, width_f), BF16),
            pltpu.VMEM((1, row_dev), jnp.int32),
            pltpu.VMEM((1, variants), jnp.int32),
            pltpu.SemaphoreType.DMA((4,)),
        ],
        compiler_params=params(60),
        name="split_rows",
    )(hidden, row_variant.reshape(1, row_dev), variant_slot.reshape(1, variants))
    x = lax.all_to_all(outgoing, "cols", 0, 0)

    slots, place = pl.pallas_call(
        functools.partial(route_kernel, plan, capacity),
        out_shape=(
            jax.ShapeDtypeStruct((peers, local_slots, window), BF16),
            jax.ShapeDtypeStruct((all_rows, 1), jnp.int32),
        ),
        in_specs=[smem, vmem],
        compiler_params=params(),
        name="route",
    )(scal, x)
    arrived = lax.all_to_all(slots, "cols", 0, 0)
    x, place = lax.optimization_barrier((x, place))

    tile = min(512, width_d)
    keep, send = pl.pallas_call(
        functools.partial(base_kernel, plan),
        grid=(width_d // tile,),
        out_shape=(
            jax.ShapeDtypeStruct((half, row_dev, width_d), F32),
            jax.ShapeDtypeStruct((half, row_dev, width_d), BF16),
        ),
        in_specs=[
            smem,
            pl.BlockSpec((peers, row_dev, window), lambda t: (0, 0, 0)),
            pl.BlockSpec((share, tile), lambda t: (0, t)),
        ],
        out_specs=(
            pl.BlockSpec((half, row_dev, tile), lambda t: (0, 0, t)),
            pl.BlockSpec((half, row_dev, tile), lambda t: (0, 0, t)),
        ),
        scratch_shapes=[pltpu.VMEM((all_rows, share), BF16)],
        compiler_params=params(),
        cost_estimate=pl.CostEstimate(
            flops=2 * all_rows * share * width_d,
            bytes_accessed=2 * share * width_d + 6 * all_rows // 2 * width_d,
            transcendentals=0,
        ),
        name="base",
    )(scal, x, down_weight)
    pairs = lambda step: [(i, i ^ step) for i in range(peers)]

    def halve(step, keep, got):
        bit = ((me // step) % 2).astype(jnp.int32).reshape(1)
        left = (keep.shape[0] // 2, row_dev, width_d)
        return pl.pallas_call(
            halve_kernel,
            in_specs=[smem, vmem, vmem],
            out_shape=(jax.ShapeDtypeStruct(left, F32), jax.ShapeDtypeStruct(left, BF16)),
            compiler_params=params(),
            name="halve",
        )(bit, keep, got)

    got = lax.ppermute(send, "cols", pairs(1))
    step = 2
    if step < peers:
        keep, send = halve(step, keep, got)
        send, arrived = lax.optimization_barrier((send, arrived))

    group = split_factor(count, 64)
    aligned = slice_d % LANES == 0
    shape = (peers, local_slots, slice_d) if aligned else (local_slots, width_d)
    chunks = local_var * (count // group)
    deltas = pl.pallas_call(
        functools.partial(delta_kernel, plan, d_blocks, group),
        in_specs=[smem, vmem, anywhere],
        out_specs=vmem,
        scratch_shapes=[
            pltpu.VMEM((local_var, f_blocks, capacity, block_size), F32),
            pltpu.VMEM((local_var, d_blocks, capacity, block_size), F32),
            pltpu.VMEM((chunks, group, block_size, block_size), BF16),
            pltpu.SemaphoreType.DMA((chunks,)),
        ],
        out_shape=jax.ShapeDtypeStruct(shape, BF16),
        compiler_params=params(36),
        cost_estimate=pl.CostEstimate(
            flops=2 * local_slots * count * block_size * block_size,
            bytes_accessed=2 * local_var * count * block_size * block_size,
            transcendentals=0,
        ),
        name="delta",
    )(block_ids, arrived, delta_values)
    if not aligned:
        deltas = deltas.reshape(local_slots, peers, slice_d).transpose(1, 0, 2)
    columns = lax.all_to_all(deltas, "cols", 0, 0)
    while step < peers:
        got = lax.ppermute(send, "cols", pairs(step))
        step *= 2
        if step < peers:
            keep, send = halve(step, keep, got)
        if step == peers // 2:
            send, place = lax.optimization_barrier((send, place))
    by_row = pl.pallas_call(
        pick_kernel,
        out_shape=jax.ShapeDtypeStruct((peers, row_dev, slice_d), BF16),
        compiler_params=params(),
        name="pick",
    )(place, columns)
    own = lax.all_to_all(by_row, "cols", 0, 0)
    return pl.pallas_call(
        finish_kernel,
        out_shape=jax.ShapeDtypeStruct((row_dev, width_d), BF16),
        compiler_params=params(),
        name="finish",
    )(keep, got, own)


def solution(mesh):
    return jax.shard_map(
        body,
        mesh=mesh,
        in_specs=(
            P(("groups", "cols"), None),
            P("cols", None),
            P("cols", None, None, None),
            P("cols", None),
            P(),
            P(("groups", "cols"), None),
        ),
        out_specs=P(("groups", "cols"), None),
        check_vma=False,
    )
```

```python
import functools

import jax
import jax.numpy as jnp
from jax import lax
from jax.experimental import pallas as pl
from jax.experimental.pallas import tpu as pltpu
from jax.sharding import PartitionSpec as P

LANES = 128
BF16 = jnp.bfloat16
F32 = jnp.float32


def windows(width_f, peers):
    share = width_f // peers
    most = max((s * share) % LANES for s in range(peers))
    window = -(-(share + most) // LANES) * LANES
    if window == share:
        window += LANES
    last = (width_f - window) // LANES
    starts = [min(s * share // LANES, last) for s in range(peers)]
    return share, window, last, starts


def params(mib=16):
    return pltpu.CompilerParams(vmem_limit_bytes=mib * 1024 * 1024)


def lane_iota(rows, lanes):
    return lax.broadcasted_iota(jnp.int32, (rows, lanes), 1)


def split_kernel(plan, h_hbm, id_hbm, slot_hbm, o_ref, h_ref, id_ref, slot_ref, sems):
    share, window, _, starts = plan
    rows, width = h_ref.shape
    variants = slot_ref.shape[1]
    cut = width // LANES // 2 * LANES
    halves = (slice(0, cut), slice(cut, width))
    copies = [
        pltpu.make_async_copy(id_hbm, id_ref, sems.at[0]),
        pltpu.make_async_copy(slot_hbm, slot_ref, sems.at[1]),
        pltpu.make_async_copy(h_hbm.at[:, halves[0]], h_ref.at[:, halves[0]], sems.at[2]),
        pltpu.make_async_copy(h_hbm.at[:, halves[1]], h_ref.at[:, halves[1]], sems.at[3]),
    ]
    for copy in copies:
        copy.start()
    copies[0].wait()
    copies[1].wait()
    lane = lane_iota(rows, window)
    diagonal = lax.broadcasted_iota(jnp.int32, (rows, rows), 0) == lane_iota(rows, rows)
    ids = jnp.sum(jnp.where(diagonal, id_ref[...].astype(F32), 0.0), axis=1, keepdims=True)
    named = ids.astype(jnp.int32) == lane_iota(rows, variants)
    slot = jnp.sum(jnp.where(named, slot_ref[...].astype(F32), 0.0), axis=1, keepdims=True)
    copies[2].wait()
    late = True
    for s, b in enumerate(starts):
        if late and b * LANES + window > cut:
            copies[3].wait()
            late = False
        spare = (s * share - b * LANES + share) % window
        piece = h_ref[:, b * LANES : b * LANES + window].astype(F32)
        o_ref[s] = jnp.where(lane == spare, slot, piece).astype(BF16)


def own_shift(plan):
    share, _, last, _ = plan
    start = lax.axis_index("cols") * share
    return start - jnp.minimum(start // LANES, last) * LANES


def route_kernel(plan, capacity, shift_ref, x_ref, o_ref, place_ref):
    share, window, _, _ = plan
    peers, row_dev, _ = x_ref.shape
    rows = peers * row_dev
    slots = o_ref.shape[0] * o_ref.shape[1]
    variants = slots // capacity
    spare = lax.rem(shift_ref[0] + share, window)
    tile = pl.multiple_of(spare // LANES * LANES, LANES)
    near = x_ref[:, :, pl.ds(tile, LANES)].reshape(rows, LANES).astype(F32)
    at = lane_iota(rows, LANES) == spare - tile
    slot = jnp.sum(jnp.where(at, near, 0.0), axis=1, keepdims=True)
    data = x_ref[...].reshape(rows, window)
    onehot = jnp.where(slot.astype(jnp.int32) == lane_iota(rows, variants), 1.0, 0.0)
    row_i = lax.broadcasted_iota(jnp.int32, (rows, rows), 0)
    row_j = lane_iota(rows, rows)
    earlier = jnp.where(row_j < row_i, 1.0, 0.0).astype(BF16)
    before = jnp.dot(earlier, onehot.astype(BF16), preferred_element_type=F32)
    rank = jnp.sum(before * onehot, axis=1, keepdims=True)
    place = slot * capacity + rank
    place_ref[...] = place.astype(jnp.int32)
    across = jnp.sum(jnp.where(row_i == row_j, place, 0.0), axis=0, keepdims=True)
    pick = across.astype(jnp.int32) == lax.broadcasted_iota(jnp.int32, (slots, rows), 0)
    pick = jnp.where(pick, 1.0, 0.0).astype(BF16)
    filled = jnp.dot(pick, data, preferred_element_type=F32).astype(BF16)
    o_ref[...] = filled.reshape(o_ref.shape)


def base_kernel(plan, scal_ref, x_ref, w_hbm, keep_ref, send_ref, mine_ref, w_ref, sems):
    share, window, _, _ = plan
    peers, row_dev, _ = x_ref.shape
    half = peers // 2 * row_dev
    parts, _, cols = w_ref.shape

    def fetch(p):
        return pltpu.make_async_copy(w_hbm.at[:, pl.ds(p * cols, cols)], w_ref.at[p], sems.at[p])

    for p in range(parts):
        fetch(p).start()
    bit = scal_ref[1]
    for side in (0, 1):
        which = bit if side == 0 else 1 - bit
        for q in range(peers // 2):
            piece = x_ref[2 * q + which].astype(F32)
            piece = pltpu.roll(piece, window - scal_ref[0], 1)
            at = side * half + q * row_dev
            mine_ref[at : at + row_dev] = piece[:, :share].astype(BF16)
    for p in range(parts):
        fetch(p).wait()
        both = jnp.dot(mine_ref[...], w_ref[p], preferred_element_type=F32)
        at = slice(p * cols, (p + 1) * cols)
        keep_ref[:, :, at] = both[:half].reshape(keep_ref.shape[:2] + (cols,))
        send_ref[:, :, at] = both[half:].astype(BF16).reshape(send_ref.shape[:2] + (cols,))


def delta_kernel(plan, d_blocks, group, ids_ref, x_ref, v_hbm, o_ref, rows_ref, acc_ref, held_ref, sems):
    share, window, _, starts = plan
    local_var, f_blocks, capacity, _ = rows_ref.shape
    chunks, _, size, _ = held_ref.shape
    per = chunks // local_var

    def fetch(c):
        source = v_hbm.at[c // per, pl.ds((c % per) * group, group)]
        return pltpu.make_async_copy(source, held_ref.at[c], sems.at[c])

    for c in range(chunks):
        fetch(c).start()

    acc_ref[...] = jnp.zeros_like(acc_ref)
    done = set()
    for s, b in enumerate(starts):
        for k in range(window // LANES):
            tile = x_ref[s, :, k * LANES : (k + 1) * LANES].astype(F32)
            low = s * share - (b + k) * LANES
            if low > 0 or low + share < LANES:
                lane = lane_iota(tile.shape[0], LANES)
                tile = jnp.where((lane >= low) & (lane < low + share), tile, 0.0)
            for v in range(local_var):
                part = tile[v * capacity : (v + 1) * capacity]
                if b + k in done:
                    part = part + rows_ref[v, b + k]
                rows_ref[v, b + k] = part
            done.add(b + k)

    zeros = jnp.zeros((capacity, size), F32)

    def one_chunk(c, carry):
        var = lax.div(c, per)
        first = lax.rem(c, per) * group
        pltpu.make_async_copy(
            v_hbm.at[var, pl.ds(first, group)], held_ref.at[c], sems.at[c]
        ).wait()
        sums = []
        for n in range(0, group, 2):
            blocks = [ids_ref[var, first + m] for m in range(n, min(n + 2, group))]
            lhs = [rows_ref[var, lax.div(block, d_blocks)] for block in blocks]
            if len(blocks) == 2:
                upper = jnp.concatenate([lhs[0], zeros], axis=1)
                lower = jnp.concatenate([zeros, lhs[1]], axis=1)
                left = jnp.concatenate([upper, lower], axis=0).astype(BF16)
                right = held_ref[c, n : n + 2].reshape(2 * size, size)
            else:
                left = lhs[0].astype(BF16)
                right = held_ref[c, n]
            product = jnp.dot(left, right, preferred_element_type=F32)
            for q, block in enumerate(blocks):
                part = product[q * capacity : (q + 1) * capacity]
                sums.append((lax.rem(block, d_blocks), part))
        for column, part in sums:
            acc_ref[var, column] += part
        return carry

    lax.fori_loop(0, chunks, one_chunk, 0)
    for j in range(d_blocks):
        whole = jnp.concatenate([acc_ref[v, j] for v in range(local_var)], axis=0)
        if len(o_ref.shape) == 3:
            per_peer = o_ref.shape[2] // LANES
            k = j % per_peer
            o_ref[j // per_peer, :, k * LANES : (k + 1) * LANES] = whole.astype(BF16)
        else:
            o_ref[:, j * LANES : (j + 1) * LANES] = whole.astype(BF16)


def pick_kernel(place_ref, c_ref, o_ref):
    peers, per_owner, cols = c_ref.shape
    slots = peers * per_owner
    rows = place_ref.shape[0]
    pick = place_ref[...] == lane_iota(rows, slots)
    pick = jnp.where(pick, 1.0, 0.0).astype(BF16)
    found = jnp.dot(pick, c_ref[...].reshape(slots, cols), preferred_element_type=F32)
    o_ref[...] = found.astype(BF16).reshape(o_ref.shape)


def halve_kernel(bit_ref, keep_ref, got_ref, next_ref, send_ref):
    bit = bit_ref[0]
    for q in range(next_ref.shape[0]):
        mine, other = 2 * q + bit, 2 * q + 1 - bit
        next_ref[q] = keep_ref[mine] + got_ref[mine].astype(F32)
        send_ref[q] = (keep_ref[other] + got_ref[other].astype(F32)).astype(BF16)


def finish_kernel(keep_ref, got_ref, own_ref, o_ref):
    peers, _, cols = own_ref.shape
    base = keep_ref[0] + got_ref[0].astype(F32)
    if cols % LANES == 0:
        for s in range(peers):
            at = slice(s * cols, (s + 1) * cols)
            o_ref[:, at] = (base[:, at] + own_ref[s].astype(F32)).astype(BF16)
    else:
        own = jnp.concatenate([own_ref[s].astype(F32) for s in range(peers)], axis=1)
        o_ref[...] = (base + own).astype(BF16)


def split_factor(count, most):
    return max(g for g in range(1, most + 1) if count % g == 0)


def body(hidden, down_weight, delta_values, block_ids, variant_slot, row_variant):
    peers = lax.axis_size("cols")
    me = lax.axis_index("cols")
    row_dev, width_f = hidden.shape
    width_d = down_weight.shape[1]
    local_var, count, block_size, _ = delta_values.shape
    variants = variant_slot.shape[0]
    all_rows = row_dev * peers
    capacity = 2 * all_rows // variants
    d_blocks = width_d // block_size
    f_blocks = width_f // block_size
    local_slots = local_var * capacity
    plan = windows(width_f, peers)
    share, window, _, _ = plan
    half = peers // 2
    slice_d = width_d // peers

    scal = jnp.stack([own_shift(plan), me % 2]).astype(jnp.int32)
    smem = pl.BlockSpec(memory_space=pltpu.SMEM)
    vmem = pl.BlockSpec(memory_space=pltpu.VMEM)
    anywhere = pl.BlockSpec(memory_space=pl.ANY)

    outgoing = pl.pallas_call(
        functools.partial(split_kernel, plan),
        in_specs=[anywhere] * 3,
        out_shape=jax.ShapeDtypeStruct((peers, row_dev, window), BF16),
        scratch_shapes=[
            pltpu.VMEM((row_dev, width_f), BF16),
            pltpu.VMEM((1, row_dev), jnp.int32),
            pltpu.VMEM((1, variants), jnp.int32),
            pltpu.SemaphoreType.DMA((4,)),
        ],
        compiler_params=params(60),
        name="split_rows",
    )(hidden, row_variant.reshape(1, row_dev), variant_slot.reshape(1, variants))
    x = lax.all_to_all(outgoing, "cols", 0, 0)

    slots, place = pl.pallas_call(
        functools.partial(route_kernel, plan, capacity),
        out_shape=(
            jax.ShapeDtypeStruct((peers, local_slots, window), BF16),
            jax.ShapeDtypeStruct((all_rows, 1), jnp.int32),
        ),
        in_specs=[smem, vmem],
        compiler_params=params(),
        name="route",
    )(scal, x)
    arrived = lax.all_to_all(slots, "cols", 0, 0)
    x, place = lax.optimization_barrier((x, place))

    cols = min(512, width_d)
    part = (half, row_dev, width_d)
    keep, send = pl.pallas_call(
        functools.partial(base_kernel, plan),
        in_specs=[smem, vmem, anywhere],
        out_specs=(vmem, vmem),
        out_shape=(jax.ShapeDtypeStruct(part, F32), jax.ShapeDtypeStruct(part, BF16)),
        scratch_shapes=[
            pltpu.VMEM((all_rows, share), BF16),
            pltpu.VMEM((width_d // cols, share, cols), BF16),
            pltpu.SemaphoreType.DMA((width_d // cols,)),
        ],
        compiler_params=params(48),
        cost_estimate=pl.CostEstimate(
            flops=2 * all_rows * share * width_d,
            bytes_accessed=2 * share * width_d,
            transcendentals=0,
        ),
        name="base",
    )(scal, x, down_weight)
    pairs = lambda step: [(i, i ^ step) for i in range(peers)]

    def halve(step, keep, got):
        bit = ((me // step) % 2).astype(jnp.int32).reshape(1)
        left = (keep.shape[0] // 2, row_dev, width_d)
        return pl.pallas_call(
            halve_kernel,
            in_specs=[smem, vmem, vmem],
            out_shape=(jax.ShapeDtypeStruct(left, F32), jax.ShapeDtypeStruct(left, BF16)),
            compiler_params=params(60 if step == 2 else 16),
            name="halve",
        )(bit, keep, got)

    got = lax.ppermute(send, "cols", pairs(1))
    step = 2
    if step < peers:
        keep, send = halve(step, keep, got)

    group = split_factor(count, 64)
    aligned = slice_d % LANES == 0
    shape = (peers, local_slots, slice_d) if aligned else (local_slots, width_d)
    chunks = local_var * (count // group)
    deltas = pl.pallas_call(
        functools.partial(delta_kernel, plan, d_blocks, group),
        in_specs=[smem, vmem, anywhere],
        out_specs=vmem,
        scratch_shapes=[
            pltpu.VMEM((local_var, f_blocks, capacity, block_size), F32),
            pltpu.VMEM((local_var, d_blocks, capacity, block_size), F32),
            pltpu.VMEM((chunks, group, block_size, block_size), BF16),
            pltpu.SemaphoreType.DMA((chunks,)),
        ],
        out_shape=jax.ShapeDtypeStruct(shape, BF16),
        compiler_params=params(36),
        cost_estimate=pl.CostEstimate(
            flops=2 * local_slots * count * block_size * block_size,
            bytes_accessed=2 * local_var * count * block_size * block_size,
            transcendentals=0,
        ),
        name="delta",
    )(block_ids, arrived, delta_values)
    if not aligned:
        deltas = deltas.reshape(local_slots, peers, slice_d).transpose(1, 0, 2)
    columns = lax.all_to_all(deltas, "cols", 0, 0)
    while step < peers:
        got = lax.ppermute(send, "cols", pairs(step))
        step *= 2
        if step < peers:
            keep, send = halve(step, keep, got)
    by_row = pl.pallas_call(
        pick_kernel,
        out_shape=jax.ShapeDtypeStruct((peers, row_dev, slice_d), BF16),
        compiler_params=params(),
        name="pick",
    )(place, columns)
    own = lax.all_to_all(by_row, "cols", 0, 0)
    return pl.pallas_call(
        finish_kernel,
        out_shape=jax.ShapeDtypeStruct((row_dev, width_d), BF16),
        compiler_params=params(),
        name="finish",
    )(keep, got, own)


def solution(mesh):
    return jax.shard_map(
        body,
        mesh=mesh,
        in_specs=(
            P(("groups", "cols"), None),
            P("cols", None),
            P("cols", None, None, None),
            P("cols", None),
            P(),
            P(("groups", "cols"), None),
        ),
        out_specs=P(("groups", "cols"), None),
        check_vma=False,
    )
```

```python
import functools

import jax
import jax.numpy as jnp
from jax import lax
from jax.experimental import pallas as pl
from jax.experimental.pallas import tpu as pltpu
from jax.sharding import PartitionSpec as P

LANES = 128
BF16 = jnp.bfloat16
F32 = jnp.float32


def windows(width_f, peers):
    share = width_f // peers
    most = max((s * share) % LANES for s in range(peers))
    window = -(-(share + most) // LANES) * LANES
    if window == share:
        window += LANES
    last = (width_f - window) // LANES
    starts = [min(s * share // LANES, last) for s in range(peers)]
    return share, window, last, starts


def params(mib=16):
    return pltpu.CompilerParams(vmem_limit_bytes=mib * 1024 * 1024)


def lane_iota(rows, lanes):
    return lax.broadcasted_iota(jnp.int32, (rows, lanes), 1)


def split_kernel(plan, h_hbm, id_hbm, slot_hbm, o_ref, h_ref, id_ref, slot_ref, sems):
    share, window, _, starts = plan
    rows, width = h_ref.shape
    variants = slot_ref.shape[1]
    cut = width // LANES // 2 * LANES
    halves = (slice(0, cut), slice(cut, width))
    copies = [
        pltpu.make_async_copy(id_hbm, id_ref, sems.at[0]),
        pltpu.make_async_copy(slot_hbm, slot_ref, sems.at[1]),
        pltpu.make_async_copy(h_hbm.at[:, halves[0]], h_ref.at[:, halves[0]], sems.at[2]),
        pltpu.make_async_copy(h_hbm.at[:, halves[1]], h_ref.at[:, halves[1]], sems.at[3]),
    ]
    for copy in copies:
        copy.start()
    copies[0].wait()
    copies[1].wait()
    lane = lane_iota(rows, window)
    diagonal = lax.broadcasted_iota(jnp.int32, (rows, rows), 0) == lane_iota(rows, rows)
    ids = jnp.sum(jnp.where(diagonal, id_ref[...].astype(F32), 0.0), axis=1, keepdims=True)
    named = ids.astype(jnp.int32) == lane_iota(rows, variants)
    slot = jnp.sum(jnp.where(named, slot_ref[...].astype(F32), 0.0), axis=1, keepdims=True)
    copies[2].wait()
    late = True
    for s, b in enumerate(starts):
        if late and b * LANES + window > cut:
            copies[3].wait()
            late = False
        spare = (s * share - b * LANES + share) % window
        piece = h_ref[:, b * LANES : b * LANES + window].astype(F32)
        o_ref[s] = jnp.where(lane == spare, slot, piece).astype(BF16)


def own_shift(plan):
    share, _, last, _ = plan
    start = lax.axis_index("cols") * share
    return start - jnp.minimum(start // LANES, last) * LANES


def route_kernel(plan, capacity, shift_ref, x_ref, o_ref, place_ref):
    share, window, _, _ = plan
    peers, row_dev, _ = x_ref.shape
    rows = peers * row_dev
    slots = o_ref.shape[0] * o_ref.shape[1]
    variants = slots // capacity
    spare = lax.rem(shift_ref[0] + share, window)
    tile = pl.multiple_of(spare // LANES * LANES, LANES)
    near = x_ref[:, :, pl.ds(tile, LANES)].reshape(rows, LANES).astype(F32)
    at = lane_iota(rows, LANES) == spare - tile
    slot = jnp.sum(jnp.where(at, near, 0.0), axis=1, keepdims=True)
    data = x_ref[...].reshape(rows, window)
    onehot = jnp.where(slot.astype(jnp.int32) == lane_iota(rows, variants), 1.0, 0.0)
    row_i = lax.broadcasted_iota(jnp.int32, (rows, rows), 0)
    row_j = lane_iota(rows, rows)
    earlier = jnp.where(row_j < row_i, 1.0, 0.0).astype(BF16)
    before = jnp.dot(earlier, onehot.astype(BF16), preferred_element_type=F32)
    rank = jnp.sum(before * onehot, axis=1, keepdims=True)
    place = slot * capacity + rank
    place_ref[...] = place.astype(jnp.int32)
    across = jnp.sum(jnp.where(row_i == row_j, place, 0.0), axis=0, keepdims=True)
    pick = across.astype(jnp.int32) == lax.broadcasted_iota(jnp.int32, (slots, rows), 0)
    pick = jnp.where(pick, 1.0, 0.0).astype(BF16)
    filled = jnp.dot(pick, data, preferred_element_type=F32).astype(BF16)
    o_ref[...] = filled.reshape(o_ref.shape)


def base_kernel(plan, scal_ref, x_ref, w_hbm, keep_ref, send_ref, mine_ref, w_ref, sems):
    share, window, _, _ = plan
    peers, row_dev, _ = x_ref.shape
    half = peers // 2 * row_dev
    parts, _, cols = w_ref.shape

    def fetch(p):
        return pltpu.make_async_copy(w_hbm.at[:, pl.ds(p * cols, cols)], w_ref.at[p], sems.at[p])

    for p in range(parts):
        fetch(p).start()
    bit = scal_ref[1]
    for side in (0, 1):
        which = bit if side == 0 else 1 - bit
        for q in range(peers // 2):
            piece = x_ref[2 * q + which].astype(F32)
            piece = pltpu.roll(piece, window - scal_ref[0], 1)
            at = side * half + q * row_dev
            mine_ref[at : at + row_dev] = piece[:, :share].astype(BF16)
    for p in range(parts):
        fetch(p).wait()
        both = jnp.dot(mine_ref[...], w_ref[p], preferred_element_type=F32)
        at = slice(p * cols, (p + 1) * cols)
        keep_ref[:, :, at] = both[:half].reshape(keep_ref.shape[:2] + (cols,))
        send_ref[:, :, at] = both[half:].astype(BF16).reshape(send_ref.shape[:2] + (cols,))


def delta_kernel(plan, d_blocks, group, ids_ref, x_ref, v_hbm, o_ref, rows_ref, acc_ref, held_ref, sems):
    share, window, _, starts = plan
    local_var, f_blocks, capacity, _ = rows_ref.shape
    chunks, _, size, _ = held_ref.shape
    per = chunks // local_var

    def fetch(c):
        source = v_hbm.at[c // per, pl.ds((c % per) * group, group)]
        return pltpu.make_async_copy(source, held_ref.at[c], sems.at[c])

    for c in range(chunks):
        fetch(c).start()

    acc_ref[...] = jnp.zeros_like(acc_ref)
    done = set()
    for s, b in enumerate(starts):
        for k in range(window // LANES):
            tile = x_ref[s, :, k * LANES : (k + 1) * LANES].astype(F32)
            low = s * share - (b + k) * LANES
            if low > 0 or low + share < LANES:
                lane = lane_iota(tile.shape[0], LANES)
                tile = jnp.where((lane >= low) & (lane < low + share), tile, 0.0)
            for v in range(local_var):
                part = tile[v * capacity : (v + 1) * capacity]
                if b + k in done:
                    part = part + rows_ref[v, b + k]
                rows_ref[v, b + k] = part
            done.add(b + k)

    zeros = jnp.zeros((capacity, size), F32)

    def one_chunk(c, carry):
        var = lax.div(c, per)
        first = lax.rem(c, per) * group
        pltpu.make_async_copy(
            v_hbm.at[var, pl.ds(first, group)], held_ref.at[c], sems.at[c]
        ).wait()
        sums = []
        for n in range(0, group, 2):
            blocks = [ids_ref[var, first + m] for m in range(n, min(n + 2, group))]
            lhs = [rows_ref[var, lax.div(block, d_blocks)] for block in blocks]
            if len(blocks) == 2:
                upper = jnp.concatenate([lhs[0], zeros], axis=1)
                lower = jnp.concatenate([zeros, lhs[1]], axis=1)
                left = jnp.concatenate([upper, lower], axis=0).astype(BF16)
                right = held_ref[c, n : n + 2].reshape(2 * size, size)
            else:
                left = lhs[0].astype(BF16)
                right = held_ref[c, n]
            product = jnp.dot(left, right, preferred_element_type=F32)
            for q, block in enumerate(blocks):
                part = product[q * capacity : (q + 1) * capacity]
                sums.append((lax.rem(block, d_blocks), part))
        for column, part in sums:
            acc_ref[var, column] += part
        return carry

    lax.fori_loop(0, chunks, one_chunk, 0)
    for j in range(d_blocks):
        whole = jnp.concatenate([acc_ref[v, j] for v in range(local_var)], axis=0)
        o_ref[:, j * LANES : (j + 1) * LANES] = whole.astype(BF16)


def pair_kernel(keep_ref, got_ref, o_ref):
    o_ref[...] = keep_ref[...] + got_ref[...].astype(F32)


def join_kernel(stride, scal_ref, bit_ref, base_ref, place_ref, own_ref, got_ref, *rest):
    next_ref, send_ref, sum_ref = rest
    rows = place_ref.shape[0]
    slots, cols = own_ref.shape
    lane = lane_iota(rows, slots)
    for source, (first, d_ref) in enumerate(((scal_ref[2], own_ref), (scal_ref[3], got_ref))):
        pick = jnp.where(place_ref[...] - first == lane, 1.0, 0.0).astype(BF16)
        part = jnp.dot(pick, d_ref[...], preferred_element_type=F32).reshape(sum_ref.shape)
        if source == 0:
            sum_ref[...] = base_ref[...] + part
        else:
            sum_ref[...] += part
    bit = bit_ref[0]
    for q in range(next_ref.shape[0]):
        at = q // stride * 2 * stride + q % stride
        next_ref[q] = sum_ref[at + stride * bit]
        send_ref[q] = sum_ref[at + stride * (1 - bit)].astype(BF16)


def halve_kernel(stride, bit_ref, keep_ref, got_ref, next_ref, send_ref):
    bit = bit_ref[0]
    for q in range(next_ref.shape[0]):
        first = q // stride * 2 * stride + q % stride
        mine, other = first + stride * bit, first + stride * (1 - bit)
        next_ref[q] = keep_ref[mine] + got_ref[mine].astype(F32)
        send_ref[q] = (keep_ref[other] + got_ref[other].astype(F32)).astype(BF16)


def finish_kernel(*refs):
    o_ref = refs[-1]
    cols = o_ref.shape[1] // 2
    for side in (0, 1):
        keep_ref, got_ref = refs[2 * side : 2 * side + 2]
        total = keep_ref[0] + got_ref[0].astype(F32)
        o_ref[:, side * cols : (side + 1) * cols] = total.astype(BF16)


def split_factor(count, most):
    return max(g for g in range(1, most + 1) if count % g == 0)


def body(hidden, down_weight, delta_values, block_ids, variant_slot, row_variant):
    peers = lax.axis_size("cols")
    me = lax.axis_index("cols")
    row_dev, width_f = hidden.shape
    width_d = down_weight.shape[1]
    local_var, count, block_size, _ = delta_values.shape
    variants = variant_slot.shape[0]
    all_rows = row_dev * peers
    capacity = 2 * all_rows // variants
    d_blocks = width_d // block_size
    f_blocks = width_f // block_size
    local_slots = local_var * capacity
    plan = windows(width_f, peers)
    share, window, _, _ = plan
    half = peers // 2

    firsts = [me * local_slots, (me ^ 1) * local_slots]
    scal = jnp.stack([own_shift(plan), me % 2] + firsts).astype(jnp.int32)
    smem = pl.BlockSpec(memory_space=pltpu.SMEM)
    vmem = pl.BlockSpec(memory_space=pltpu.VMEM)
    anywhere = pl.BlockSpec(memory_space=pl.ANY)

    outgoing = pl.pallas_call(
        functools.partial(split_kernel, plan),
        in_specs=[anywhere] * 3,
        out_shape=jax.ShapeDtypeStruct((peers, row_dev, window), BF16),
        scratch_shapes=[
            pltpu.VMEM((row_dev, width_f), BF16),
            pltpu.VMEM((1, row_dev), jnp.int32),
            pltpu.VMEM((1, variants), jnp.int32),
            pltpu.SemaphoreType.DMA((4,)),
        ],
        compiler_params=params(60),
        name="split_rows",
    )(hidden, row_variant.reshape(1, row_dev), variant_slot.reshape(1, variants))
    x = lax.all_to_all(outgoing, "cols", 0, 0)

    slots, place = pl.pallas_call(
        functools.partial(route_kernel, plan, capacity),
        out_shape=(
            jax.ShapeDtypeStruct((peers, local_slots, window), BF16),
            jax.ShapeDtypeStruct((all_rows, 1), jnp.int32),
        ),
        in_specs=[smem, vmem],
        compiler_params=params(),
        name="route",
    )(scal, x)
    arrived = lax.all_to_all(slots, "cols", 0, 0)
    x, place = lax.optimization_barrier((x, place))

    cols = min(512, width_d)
    part = (half, row_dev, width_d)
    keep, send = pl.pallas_call(
        functools.partial(base_kernel, plan),
        in_specs=[smem, vmem, anywhere],
        out_specs=(vmem, vmem),
        out_shape=(jax.ShapeDtypeStruct(part, F32), jax.ShapeDtypeStruct(part, BF16)),
        scratch_shapes=[
            pltpu.VMEM((all_rows, share), BF16),
            pltpu.VMEM((width_d // cols, share, cols), BF16),
            pltpu.SemaphoreType.DMA((width_d // cols,)),
        ],
        compiler_params=params(48),
        cost_estimate=pl.CostEstimate(
            flops=2 * all_rows * share * width_d,
            bytes_accessed=2 * share * width_d,
            transcendentals=0,
        ),
        name="base",
    )(scal, x, down_weight)
    pairs = lambda step: [(i, i ^ step) for i in range(peers)]
    base = pl.pallas_call(
        pair_kernel,
        out_shape=jax.ShapeDtypeStruct(keep.shape, F32),
        compiler_params=params(60),
        name="pair",
    )(keep, lax.ppermute(send, "cols", pairs(1)))
    base, arrived = lax.optimization_barrier((base, arrived))
    place = lax.dynamic_index_in_dim(place.reshape(half, 2, row_dev, 1), me % 2, 1, keepdims=False)
    place = place.reshape(half * row_dev, 1)

    group = split_factor(count, 64)
    shape = (local_slots, width_d)
    chunks = local_var * (count // group)
    deltas = pl.pallas_call(
        functools.partial(delta_kernel, plan, d_blocks, group),
        in_specs=[smem, vmem, anywhere],
        out_specs=vmem,
        scratch_shapes=[
            pltpu.VMEM((local_var, f_blocks, capacity, block_size), F32),
            pltpu.VMEM((local_var, d_blocks, capacity, block_size), F32),
            pltpu.VMEM((chunks, group, block_size, block_size), BF16),
            pltpu.SemaphoreType.DMA((chunks,)),
        ],
        out_shape=jax.ShapeDtypeStruct(shape, BF16),
        compiler_params=params(36),
        cost_estimate=pl.CostEstimate(
            flops=2 * local_slots * count * block_size * block_size,
            bytes_accessed=2 * local_var * count * block_size * block_size,
            transcendentals=0,
        ),
        name="delta",
    )(block_ids, arrived, delta_values)
    others = lax.ppermute(deltas, "cols", pairs(1))

    cols = width_d // 2
    above = [1 << k for k in range(1, peers.bit_length() - 1)]
    ends = []
    for side, order in enumerate((above, above[1:] + above[:1])):
        open_bits = list(above)
        for count, step in enumerate(order):
            stride = 1 << open_bits.index(step)
            open_bits.remove(step)
            bit = ((me // step) % 2).astype(jnp.int32).reshape(1)
            left = (half >> (count + 1), row_dev, cols)
            outs = (jax.ShapeDtypeStruct(left, F32), jax.ShapeDtypeStruct(left, BF16))
            if count == 0:
                whole = lambda shape: pl.BlockSpec(shape, lambda i: (0,) * len(shape))
                part = lambda shape, n=side: pl.BlockSpec(shape, lambda i: (0,) * (len(shape) - 1) + (n,))
                keep, send = pl.pallas_call(
                    functools.partial(join_kernel, stride),
                    grid=(1,),
                    in_specs=[
                        smem,
                        smem,
                        part((half, row_dev, cols)),
                        whole(place.shape),
                        part((local_slots, cols)),
                        part((local_slots, cols)),
                    ],
                    out_specs=(whole(left), whole(left)),
                    out_shape=outs,
                    scratch_shapes=[pltpu.VMEM((half, row_dev, cols), F32)],
                    compiler_params=params(32),
                    name="join",
                )(scal, bit, base, place, deltas, others)
            else:
                keep, send = pl.pallas_call(
                    functools.partial(halve_kernel, stride),
                    in_specs=[smem, vmem, vmem],
                    out_shape=outs,
                    compiler_params=params(),
                    name="halve",
                )(bit, keep, got)
            got = lax.ppermute(send, "cols", pairs(step))
        ends += [keep, got]
    return pl.pallas_call(
        finish_kernel,
        out_shape=jax.ShapeDtypeStruct((row_dev, width_d), BF16),
        compiler_params=params(),
        name="finish",
    )(*ends)


def solution(mesh):
    return jax.shard_map(
        body,
        mesh=mesh,
        in_specs=(
            P(("groups", "cols"), None),
            P("cols", None),
            P("cols", None, None, None),
            P("cols", None),
            P(),
            P(("groups", "cols"), None),
        ),
        out_specs=P(("groups", "cols"), None),
        check_vma=False,
    )
```

```python
import functools

import jax
import jax.numpy as jnp
from jax import lax
from jax.experimental import pallas as pl
from jax.experimental.pallas import tpu as pltpu
from jax.sharding import PartitionSpec as P

LANES = 128
BF16 = jnp.bfloat16
F32 = jnp.float32


def windows(width_f, peers):
    share = width_f // peers
    most = max((s * share) % LANES for s in range(peers))
    window = -(-(share + most) // LANES) * LANES
    if window == share:
        window += LANES
    last = (width_f - window) // LANES
    starts = [min(s * share // LANES, last) for s in range(peers)]
    return share, window, last, starts


def params(mib=16):
    return pltpu.CompilerParams(vmem_limit_bytes=mib * 1024 * 1024)


def lane_iota(rows, lanes):
    return lax.broadcasted_iota(jnp.int32, (rows, lanes), 1)


def split_kernel(plan, h_hbm, id_hbm, slot_hbm, o_ref, h_ref, id_ref, slot_ref, sems):
    share, window, _, starts = plan
    rows, width = h_ref.shape
    variants = slot_ref.shape[1]
    cut = width // LANES // 2 * LANES
    halves = (slice(0, cut), slice(cut, width))
    copies = [
        pltpu.make_async_copy(id_hbm, id_ref, sems.at[0]),
        pltpu.make_async_copy(slot_hbm, slot_ref, sems.at[1]),
        pltpu.make_async_copy(h_hbm.at[:, halves[0]], h_ref.at[:, halves[0]], sems.at[2]),
        pltpu.make_async_copy(h_hbm.at[:, halves[1]], h_ref.at[:, halves[1]], sems.at[3]),
    ]
    for copy in copies:
        copy.start()
    copies[0].wait()
    copies[1].wait()
    lane = lane_iota(rows, window)
    diagonal = lax.broadcasted_iota(jnp.int32, (rows, rows), 0) == lane_iota(rows, rows)
    ids = jnp.sum(jnp.where(diagonal, id_ref[...].astype(F32), 0.0), axis=1, keepdims=True)
    named = ids.astype(jnp.int32) == lane_iota(rows, variants)
    slot = jnp.sum(jnp.where(named, slot_ref[...].astype(F32), 0.0), axis=1, keepdims=True)
    copies[2].wait()
    late = True
    for s, b in enumerate(starts):
        if late and b * LANES + window > cut:
            copies[3].wait()
            late = False
        spare = (s * share - b * LANES + share) % window
        piece = h_ref[:, b * LANES : b * LANES + window].astype(F32)
        o_ref[s] = jnp.where(lane == spare, slot, piece).astype(BF16)


def own_shift(plan):
    share, _, last, _ = plan
    start = lax.axis_index("cols") * share
    return start - jnp.minimum(start // LANES, last) * LANES


def route_kernel(plan, capacity, shift_ref, x_ref, o_ref, place_ref):
    share, window, _, _ = plan
    peers, row_dev, _ = x_ref.shape
    rows = peers * row_dev
    slots = o_ref.shape[0] * o_ref.shape[1]
    variants = slots // capacity
    spare = lax.rem(shift_ref[0] + share, window)
    tile = pl.multiple_of(spare // LANES * LANES, LANES)
    near = x_ref[:, :, pl.ds(tile, LANES)].reshape(rows, LANES).astype(F32)
    at = lane_iota(rows, LANES) == spare - tile
    slot = jnp.sum(jnp.where(at, near, 0.0), axis=1, keepdims=True)
    data = x_ref[...].reshape(rows, window)
    onehot = jnp.where(slot.astype(jnp.int32) == lane_iota(rows, variants), 1.0, 0.0)
    row_i = lax.broadcasted_iota(jnp.int32, (rows, rows), 0)
    row_j = lane_iota(rows, rows)
    earlier = jnp.where(row_j < row_i, 1.0, 0.0).astype(BF16)
    before = jnp.dot(earlier, onehot.astype(BF16), preferred_element_type=F32)
    rank = jnp.sum(before * onehot, axis=1, keepdims=True)
    place = slot * capacity + rank
    place_ref[...] = place.astype(jnp.int32)
    across = jnp.sum(jnp.where(row_i == row_j, place, 0.0), axis=0, keepdims=True)
    pick = across.astype(jnp.int32) == lax.broadcasted_iota(jnp.int32, (slots, rows), 0)
    pick = jnp.where(pick, 1.0, 0.0).astype(BF16)
    filled = jnp.dot(pick, data, preferred_element_type=F32).astype(BF16)
    o_ref[...] = filled.reshape(o_ref.shape)


def base_kernel(plan, scal_ref, x_ref, w_hbm, keep_ref, send_ref, mine_ref, w_ref, sems):
    share, window, _, _ = plan
    peers, row_dev, _ = x_ref.shape
    half = peers // 2 * row_dev
    parts, _, cols = w_ref.shape

    def fetch(p):
        return pltpu.make_async_copy(w_hbm.at[:, pl.ds(p * cols, cols)], w_ref.at[p], sems.at[p])

    for p in range(parts):
        fetch(p).start()
    bit = scal_ref[1]
    for side in (0, 1):
        which = bit if side == 0 else 1 - bit
        for q in range(peers // 2):
            piece = x_ref[2 * q + which].astype(F32)
            piece = pltpu.roll(piece, window - scal_ref[0], 1)
            at = side * half + q * row_dev
            mine_ref[at : at + row_dev] = piece[:, :share].astype(BF16)
    for p in range(parts):
        fetch(p).wait()
        both = jnp.dot(mine_ref[...], w_ref[p], preferred_element_type=F32)
        at = slice(p * cols, (p + 1) * cols)
        keep_ref[:, :, at] = both[:half].reshape(keep_ref.shape[:2] + (cols,))
        send_ref[:, :, at] = both[half:].astype(BF16).reshape(send_ref.shape[:2] + (cols,))


def delta_kernel(plan, d_blocks, group, ids_ref, x_ref, v_hbm, o_ref, rows_ref, acc_ref, held_ref, sems):
    share, window, _, starts = plan
    local_var, f_blocks, capacity, _ = rows_ref.shape
    chunks, _, size, _ = held_ref.shape
    per = chunks // local_var

    def fetch(c):
        source = v_hbm.at[c // per, pl.ds((c % per) * group, group)]
        return pltpu.make_async_copy(source, held_ref.at[c], sems.at[c])

    for c in range(chunks):
        fetch(c).start()

    acc_ref[...] = jnp.zeros_like(acc_ref)
    done = set()
    for s, b in enumerate(starts):
        for k in range(window // LANES):
            tile = x_ref[s, :, k * LANES : (k + 1) * LANES].astype(F32)
            low = s * share - (b + k) * LANES
            if low > 0 or low + share < LANES:
                lane = lane_iota(tile.shape[0], LANES)
                tile = jnp.where((lane >= low) & (lane < low + share), tile, 0.0)
            for v in range(local_var):
                part = tile[v * capacity : (v + 1) * capacity]
                if b + k in done:
                    part = part + rows_ref[v, b + k]
                rows_ref[v, b + k] = part
            done.add(b + k)

    zeros = jnp.zeros((capacity, size), F32)

    def one_chunk(c, carry):
        var = lax.div(c, per)
        first = lax.rem(c, per) * group
        pltpu.make_async_copy(
            v_hbm.at[var, pl.ds(first, group)], held_ref.at[c], sems.at[c]
        ).wait()
        sums = []
        for n in range(0, group, 2):
            blocks = [ids_ref[var, first + m] for m in range(n, min(n + 2, group))]
            lhs = [rows_ref[var, lax.div(block, d_blocks)] for block in blocks]
            if len(blocks) == 2:
                upper = jnp.concatenate([lhs[0], zeros], axis=1)
                lower = jnp.concatenate([zeros, lhs[1]], axis=1)
                left = jnp.concatenate([upper, lower], axis=0).astype(BF16)
                right = held_ref[c, n : n + 2].reshape(2 * size, size)
            else:
                left = lhs[0].astype(BF16)
                right = held_ref[c, n]
            product = jnp.dot(left, right, preferred_element_type=F32)
            for q, block in enumerate(blocks):
                part = product[q * capacity : (q + 1) * capacity]
                sums.append((lax.rem(block, d_blocks), part))
        for column, part in sums:
            acc_ref[var, column] += part
        return carry

    lax.fori_loop(0, chunks, one_chunk, 0)
    for j in range(d_blocks):
        whole = jnp.concatenate([acc_ref[v, j] for v in range(local_var)], axis=0)
        o_ref[:, j * LANES : (j + 1) * LANES] = whole.astype(BF16)


def pair_kernel(keep_ref, got_ref, o_ref):
    o_ref[...] = keep_ref[...] + got_ref[...].astype(F32)


def join_kernel(stride, first, scal_ref, bit_ref, base_ref, place_ref, own_ref, got_ref, *rest):
    next_ref, send_ref, sum_ref = rest
    rows = place_ref.shape[0]
    slots = own_ref.shape[0]
    cols = next_ref.shape[2]
    lane = lane_iota(rows, slots)
    picks = [place_ref[...] - scal_ref[k] == lane for k in (2, 3)]
    picks = [jnp.where(pick, 1.0, 0.0).astype(BF16) for pick in picks]
    step = cols // (cols // 512) if cols % 512 == 0 else cols
    for c in range(0, cols, step):
        at = slice(first + c, first + c + step)
        part = jnp.dot(picks[0], own_ref[:, at], preferred_element_type=F32)
        part += jnp.dot(picks[1], got_ref[:, at], preferred_element_type=F32)
        part = part.reshape(sum_ref.shape[:2] + (step,))
        sum_ref[:, :, c : c + step] = base_ref[:, :, at] + part
    bit = bit_ref[0]
    for q in range(next_ref.shape[0]):
        at = q // stride * 2 * stride + q % stride
        next_ref[q] = sum_ref[at + stride * bit]
        send_ref[q] = sum_ref[at + stride * (1 - bit)].astype(BF16)


def halve_kernel(stride, bit_ref, keep_ref, got_ref, next_ref, send_ref):
    bit = bit_ref[0]
    for q in range(next_ref.shape[0]):
        first = q // stride * 2 * stride + q % stride
        mine, other = first + stride * bit, first + stride * (1 - bit)
        next_ref[q] = keep_ref[mine] + got_ref[mine].astype(F32)
        send_ref[q] = (keep_ref[other] + got_ref[other].astype(F32)).astype(BF16)


def finish_kernel(*refs):
    o_ref = refs[-1]
    first = 0
    for side in (0, 1):
        keep_ref, got_ref = refs[2 * side : 2 * side + 2]
        cols = keep_ref.shape[2]
        total = keep_ref[0] + got_ref[0].astype(F32)
        o_ref[:, first : first + cols] = total.astype(BF16)
        first += cols


def split_factor(count, most):
    return max(g for g in range(1, most + 1) if count % g == 0)


def body(hidden, down_weight, delta_values, block_ids, variant_slot, row_variant):
    peers = lax.axis_size("cols")
    me = lax.axis_index("cols")
    row_dev, width_f = hidden.shape
    width_d = down_weight.shape[1]
    local_var, count, block_size, _ = delta_values.shape
    variants = variant_slot.shape[0]
    all_rows = row_dev * peers
    capacity = 2 * all_rows // variants
    d_blocks = width_d // block_size
    f_blocks = width_f // block_size
    local_slots = local_var * capacity
    plan = windows(width_f, peers)
    share, window, _, _ = plan
    half = peers // 2

    firsts = [me * local_slots, (me ^ 1) * local_slots]
    scal = jnp.stack([own_shift(plan), me % 2] + firsts).astype(jnp.int32)
    smem = pl.BlockSpec(memory_space=pltpu.SMEM)
    vmem = pl.BlockSpec(memory_space=pltpu.VMEM)
    anywhere = pl.BlockSpec(memory_space=pl.ANY)

    outgoing = pl.pallas_call(
        functools.partial(split_kernel, plan),
        in_specs=[anywhere] * 3,
        out_shape=jax.ShapeDtypeStruct((peers, row_dev, window), BF16),
        scratch_shapes=[
            pltpu.VMEM((row_dev, width_f), BF16),
            pltpu.VMEM((1, row_dev), jnp.int32),
            pltpu.VMEM((1, variants), jnp.int32),
            pltpu.SemaphoreType.DMA((4,)),
        ],
        compiler_params=params(60),
        name="split_rows",
    )(hidden, row_variant.reshape(1, row_dev), variant_slot.reshape(1, variants))
    x = lax.all_to_all(outgoing, "cols", 0, 0)

    slots, place = pl.pallas_call(
        functools.partial(route_kernel, plan, capacity),
        out_shape=(
            jax.ShapeDtypeStruct((peers, local_slots, window), BF16),
            jax.ShapeDtypeStruct((all_rows, 1), jnp.int32),
        ),
        in_specs=[smem, vmem],
        compiler_params=params(),
        name="route",
    )(scal, x)
    arrived = lax.all_to_all(slots, "cols", 0, 0)
    x, place = lax.optimization_barrier((x, place))

    cols = min(512, width_d)
    part = (half, row_dev, width_d)
    keep, send = pl.pallas_call(
        functools.partial(base_kernel, plan),
        in_specs=[smem, vmem, anywhere],
        out_specs=(vmem, vmem),
        out_shape=(jax.ShapeDtypeStruct(part, F32), jax.ShapeDtypeStruct(part, BF16)),
        scratch_shapes=[
            pltpu.VMEM((all_rows, share), BF16),
            pltpu.VMEM((width_d // cols, share, cols), BF16),
            pltpu.SemaphoreType.DMA((width_d // cols,)),
        ],
        compiler_params=params(48),
        cost_estimate=pl.CostEstimate(
            flops=2 * all_rows * share * width_d,
            bytes_accessed=2 * share * width_d,
            transcendentals=0,
        ),
        name="base",
    )(scal, x, down_weight)
    pairs = lambda step: [(i, i ^ step) for i in range(peers)]
    base = pl.pallas_call(
        pair_kernel,
        out_shape=jax.ShapeDtypeStruct(keep.shape, F32),
        compiler_params=params(60),
        name="pair",
    )(keep, lax.ppermute(send, "cols", pairs(1)))
    base, arrived = lax.optimization_barrier((base, arrived))
    place = lax.dynamic_index_in_dim(place.reshape(half, 2, row_dev, 1), me % 2, 1, keepdims=False)
    place = place.reshape(half * row_dev, 1)

    group = split_factor(count, 64)
    shape = (local_slots, width_d)
    chunks = local_var * (count // group)
    deltas = pl.pallas_call(
        functools.partial(delta_kernel, plan, d_blocks, group),
        in_specs=[smem, vmem, anywhere],
        out_specs=vmem,
        scratch_shapes=[
            pltpu.VMEM((local_var, f_blocks, capacity, block_size), F32),
            pltpu.VMEM((local_var, d_blocks, capacity, block_size), F32),
            pltpu.VMEM((chunks, group, block_size, block_size), BF16),
            pltpu.SemaphoreType.DMA((chunks,)),
        ],
        out_shape=jax.ShapeDtypeStruct(shape, BF16),
        compiler_params=params(36),
        cost_estimate=pl.CostEstimate(
            flops=2 * local_slots * count * block_size * block_size,
            bytes_accessed=2 * local_var * count * block_size * block_size,
            transcendentals=0,
        ),
        name="delta",
    )(block_ids, arrived, delta_values)
    others = lax.ppermute(deltas, "cols", pairs(1))

    tile = width_d // 8
    above = [1 << k for k in range(1, peers.bit_length() - 1)]
    ends = []
    for side, order in enumerate((above, above[1:] + above[:1])):
        first, tiles = ((0, 5), (5, 8 - 5))[side]
        cols = tiles * tile
        open_bits = list(above)
        for count, step in enumerate(order):
            stride = 1 << open_bits.index(step)
            open_bits.remove(step)
            bit = ((me // step) % 2).astype(jnp.int32).reshape(1)
            left = (half >> (count + 1), row_dev, cols)
            outs = (jax.ShapeDtypeStruct(left, F32), jax.ShapeDtypeStruct(left, BF16))
            if count == 0:
                keep, send = pl.pallas_call(
                    functools.partial(join_kernel, stride, first * tile),
                    in_specs=[smem, smem, vmem, vmem, vmem, vmem],
                    out_shape=outs,
                    scratch_shapes=[pltpu.VMEM((half, row_dev, cols), F32)],
                    compiler_params=params(12),
                    name="join",
                )(scal, bit, base, place, deltas, others)
            else:
                keep, send = pl.pallas_call(
                    functools.partial(halve_kernel, stride),
                    in_specs=[smem, vmem, vmem],
                    out_shape=outs,
                    compiler_params=params(),
                    name="halve",
                )(bit, keep, got)
            got = lax.ppermute(send, "cols", pairs(step))
        ends += [keep, got]
    return pl.pallas_call(
        finish_kernel,
        out_shape=jax.ShapeDtypeStruct((row_dev, width_d), BF16),
        compiler_params=params(),
        name="finish",
    )(*ends)


def solution(mesh):
    return jax.shard_map(
        body,
        mesh=mesh,
        in_specs=(
            P(("groups", "cols"), None),
            P("cols", None),
            P("cols", None, None, None),
            P("cols", None),
            P(),
            P(("groups", "cols"), None),
        ),
        out_specs=P(("groups", "cols"), None),
        check_vma=False,
    )
```

```python
import functools
import math

import jax
import jax.numpy as jnp
from jax import lax
from jax.experimental import pallas as pl
from jax.experimental.pallas import tpu as pltpu
from jax.sharding import PartitionSpec as P

LANES = 128
BF16 = jnp.bfloat16
F32 = jnp.float32


def windows(width_f, peers):
    share = width_f // peers
    most = max((s * share) % LANES for s in range(peers))
    window = -(-(share + most) // LANES) * LANES
    if window == share:
        window += LANES
    last = (width_f - window) // LANES
    starts = [min(s * share // LANES, last) for s in range(peers)]
    return share, window, last, starts


def params(mib=16):
    return pltpu.CompilerParams(vmem_limit_bytes=mib * 1024 * 1024)


def lane_iota(rows, lanes):
    return lax.broadcasted_iota(jnp.int32, (rows, lanes), 1)


def split_kernel(plan, h_hbm, id_hbm, slot_hbm, o_ref, h_ref, id_ref, slot_ref, sems):
    share, window, _, starts = plan
    rows, width = h_ref.shape
    variants = slot_ref.shape[1]
    cut = width // LANES // 2 * LANES
    halves = (slice(0, cut), slice(cut, width))
    copies = [
        pltpu.make_async_copy(id_hbm, id_ref, sems.at[0]),
        pltpu.make_async_copy(slot_hbm, slot_ref, sems.at[1]),
        pltpu.make_async_copy(h_hbm.at[:, halves[0]], h_ref.at[:, halves[0]], sems.at[2]),
        pltpu.make_async_copy(h_hbm.at[:, halves[1]], h_ref.at[:, halves[1]], sems.at[3]),
    ]
    for copy in copies:
        copy.start()
    copies[0].wait()
    copies[1].wait()
    lane = lane_iota(rows, window)
    diagonal = lax.broadcasted_iota(jnp.int32, (rows, rows), 0) == lane_iota(rows, rows)
    ids = jnp.sum(jnp.where(diagonal, id_ref[...].astype(F32), 0.0), axis=1, keepdims=True)
    named = ids.astype(jnp.int32) == lane_iota(rows, variants)
    slot = jnp.sum(jnp.where(named, slot_ref[...].astype(F32), 0.0), axis=1, keepdims=True)
    copies[2].wait()
    late = True
    for s, b in enumerate(starts):
        if late and b * LANES + window > cut:
            copies[3].wait()
            late = False
        spare = (s * share - b * LANES + share) % window
        piece = h_ref[:, b * LANES : b * LANES + window].astype(F32)
        o_ref[s] = jnp.where(lane == spare, slot, piece).astype(BF16)


def own_shift(plan):
    share, _, last, _ = plan
    start = lax.axis_index("cols") * share
    return start - jnp.minimum(start // LANES, last) * LANES


def route_kernel(plan, capacity, shift_ref, x_ref, o_ref, place_ref):
    share, window, _, _ = plan
    peers, row_dev, _ = x_ref.shape
    rows = peers * row_dev
    slots = o_ref.shape[0] * o_ref.shape[1]
    variants = slots // capacity
    spare = lax.rem(shift_ref[0] + share, window)
    tile = pl.multiple_of(spare // LANES * LANES, LANES)
    near = x_ref[:, :, pl.ds(tile, LANES)].reshape(rows, LANES).astype(F32)
    at = lane_iota(rows, LANES) == spare - tile
    slot = jnp.sum(jnp.where(at, near, 0.0), axis=1, keepdims=True)
    data = x_ref[...].reshape(rows, window)
    onehot = jnp.where(slot.astype(jnp.int32) == lane_iota(rows, variants), 1.0, 0.0)
    row_i = lax.broadcasted_iota(jnp.int32, (rows, rows), 0)
    row_j = lane_iota(rows, rows)
    earlier = jnp.where(row_j < row_i, 1.0, 0.0).astype(BF16)
    before = jnp.dot(earlier, onehot.astype(BF16), preferred_element_type=F32)
    rank = jnp.sum(before * onehot, axis=1, keepdims=True)
    place = slot * capacity + rank
    place_ref[...] = place.astype(jnp.int32)
    across = jnp.sum(jnp.where(row_i == row_j, place, 0.0), axis=0, keepdims=True)
    pick = across.astype(jnp.int32) == lax.broadcasted_iota(jnp.int32, (slots, rows), 0)
    pick = jnp.where(pick, 1.0, 0.0).astype(BF16)
    filled = jnp.dot(pick, data, preferred_element_type=F32).astype(BF16)
    o_ref[...] = filled.reshape(o_ref.shape)


def base_kernel(plan, scal_ref, x_ref, w_hbm, keep_ref, send_ref, mine_ref, w_ref, sems):
    share, window, _, _ = plan
    peers, row_dev, _ = x_ref.shape
    half = peers // 2 * row_dev
    parts, _, cols = w_ref.shape

    def fetch(p):
        return pltpu.make_async_copy(w_hbm.at[:, pl.ds(p * cols, cols)], w_ref.at[p], sems.at[p])

    for p in range(parts):
        fetch(p).start()
    bit = scal_ref[1]
    for side in (0, 1):
        which = bit if side == 0 else 1 - bit
        for q in range(peers // 2):
            piece = x_ref[2 * q + which].astype(F32)
            piece = pltpu.roll(piece, window - scal_ref[0], 1)
            at = side * half + q * row_dev
            mine_ref[at : at + row_dev] = piece[:, :share].astype(BF16)
    for p in range(parts):
        fetch(p).wait()
        both = jnp.dot(mine_ref[...], w_ref[p], preferred_element_type=F32)
        at = slice(p * cols, (p + 1) * cols)
        keep_ref[:, :, at] = both[:half].reshape(keep_ref.shape[:2] + (cols,))
        send_ref[:, :, at] = both[half:].astype(BF16).reshape(send_ref.shape[:2] + (cols,))


def delta_kernel(plan, d_blocks, group, ids_ref, x_ref, v_hbm, o_ref, rows_ref, acc_ref, held_ref, sems):
    share, window, _, starts = plan
    local_var, f_blocks, capacity, _ = rows_ref.shape
    chunks, _, size, _ = held_ref.shape
    per = chunks // local_var

    def fetch(c):
        source = v_hbm.at[c // per, pl.ds((c % per) * group, group)]
        return pltpu.make_async_copy(source, held_ref.at[c], sems.at[c])

    for c in range(chunks):
        fetch(c).start()

    acc_ref[...] = jnp.zeros_like(acc_ref)
    done = set()
    for s, b in enumerate(starts):
        for k in range(window // LANES):
            tile = x_ref[s, :, k * LANES : (k + 1) * LANES].astype(F32)
            low = s * share - (b + k) * LANES
            if low > 0 or low + share < LANES:
                lane = lane_iota(tile.shape[0], LANES)
                tile = jnp.where((lane >= low) & (lane < low + share), tile, 0.0)
            for v in range(local_var):
                part = tile[v * capacity : (v + 1) * capacity]
                if b + k in done:
                    part = part + rows_ref[v, b + k]
                rows_ref[v, b + k] = part
            done.add(b + k)

    zeros = jnp.zeros((capacity, size), F32)

    def one_chunk(c, carry):
        var = lax.div(c, per)
        first = lax.rem(c, per) * group
        pltpu.make_async_copy(
            v_hbm.at[var, pl.ds(first, group)], held_ref.at[c], sems.at[c]
        ).wait()
        sums = []
        for n in range(0, group, 2):
            blocks = [ids_ref[var, first + m] for m in range(n, min(n + 2, group))]
            lhs = [rows_ref[var, lax.div(block, d_blocks)] for block in blocks]
            if len(blocks) == 2:
                upper = jnp.concatenate([lhs[0], zeros], axis=1)
                lower = jnp.concatenate([zeros, lhs[1]], axis=1)
                left = jnp.concatenate([upper, lower], axis=0).astype(BF16)
                right = held_ref[c, n : n + 2].reshape(2 * size, size)
            else:
                left = lhs[0].astype(BF16)
                right = held_ref[c, n]
            product = jnp.dot(left, right, preferred_element_type=F32)
            for q, block in enumerate(blocks):
                part = product[q * capacity : (q + 1) * capacity]
                sums.append((lax.rem(block, d_blocks), part))
        for column, part in sums:
            acc_ref[var, column] += part
        return carry

    lax.fori_loop(0, chunks, one_chunk, 0)
    for j in range(d_blocks):
        whole = jnp.concatenate([acc_ref[v, j] for v in range(local_var)], axis=0)
        o_ref[:, j * LANES : (j + 1) * LANES] = whole.astype(BF16)


def pair_kernel(keep_ref, got_ref, o_ref):
    o_ref[...] = keep_ref[...] + got_ref[...].astype(F32)


def join_kernel(stride, first, scal_ref, bit_ref, base_ref, place_ref, own_ref, got_ref, *rest):
    next_ref, send_ref, sum_ref = rest
    rows = place_ref.shape[0]
    slots = own_ref.shape[0]
    cols = next_ref.shape[2]
    lane = lane_iota(rows, slots)
    picks = [place_ref[...] - scal_ref[k] == lane for k in (2, 3)]
    picks = [jnp.where(pick, 1.0, 0.0).astype(BF16) for pick in picks]
    step = math.gcd(cols, 512)
    for c in range(0, cols, step):
        at = slice(first + c, first + c + step)
        part = jnp.dot(picks[0], own_ref[:, at], preferred_element_type=F32)
        part += jnp.dot(picks[1], got_ref[:, at], preferred_element_type=F32)
        part = part.reshape(sum_ref.shape[:2] + (step,))
        sum_ref[:, :, c : c + step] = base_ref[:, :, at] + part
    bit = bit_ref[0]
    for q in range(next_ref.shape[0]):
        at = q // stride * 2 * stride + q % stride
        next_ref[q] = sum_ref[at + stride * bit]
        send_ref[q] = sum_ref[at + stride * (1 - bit)].astype(BF16)


def halve_kernel(stride, bit_ref, keep_ref, got_ref, next_ref, send_ref):
    bit = bit_ref[0]
    for q in range(next_ref.shape[0]):
        first = q // stride * 2 * stride + q % stride
        mine, other = first + stride * bit, first + stride * (1 - bit)
        next_ref[q] = keep_ref[mine] + got_ref[mine].astype(F32)
        send_ref[q] = (keep_ref[other] + got_ref[other].astype(F32)).astype(BF16)


def finish_kernel(*refs):
    o_ref = refs[-1]
    first = 0
    for side in (0, 1):
        keep_ref, got_ref = refs[2 * side : 2 * side + 2]
        cols = keep_ref.shape[2]
        total = keep_ref[0] + got_ref[0].astype(F32)
        o_ref[:, first : first + cols] = total.astype(BF16)
        first += cols


def split_factor(count, most):
    return max(g for g in range(1, most + 1) if count % g == 0)


def body(hidden, down_weight, delta_values, block_ids, variant_slot, row_variant):
    peers = lax.axis_size("cols")
    me = lax.axis_index("cols")
    row_dev, width_f = hidden.shape
    width_d = down_weight.shape[1]
    local_var, count, block_size, _ = delta_values.shape
    variants = variant_slot.shape[0]
    all_rows = row_dev * peers
    capacity = 2 * all_rows // variants
    d_blocks = width_d // block_size
    f_blocks = width_f // block_size
    local_slots = local_var * capacity
    plan = windows(width_f, peers)
    share, window, _, _ = plan
    half = peers // 2

    firsts = [me * local_slots, (me ^ 1) * local_slots]
    scal = jnp.stack([own_shift(plan), me % 2] + firsts).astype(jnp.int32)
    smem = pl.BlockSpec(memory_space=pltpu.SMEM)
    vmem = pl.BlockSpec(memory_space=pltpu.VMEM)
    anywhere = pl.BlockSpec(memory_space=pl.ANY)

    outgoing = pl.pallas_call(
        functools.partial(split_kernel, plan),
        in_specs=[anywhere] * 3,
        out_shape=jax.ShapeDtypeStruct((peers, row_dev, window), BF16),
        scratch_shapes=[
            pltpu.VMEM((row_dev, width_f), BF16),
            pltpu.VMEM((1, row_dev), jnp.int32),
            pltpu.VMEM((1, variants), jnp.int32),
            pltpu.SemaphoreType.DMA((4,)),
        ],
        compiler_params=params(60),
        name="split_rows",
    )(hidden, row_variant.reshape(1, row_dev), variant_slot.reshape(1, variants))
    x = lax.all_to_all(outgoing, "cols", 0, 0)

    slots, place = pl.pallas_call(
        functools.partial(route_kernel, plan, capacity),
        out_shape=(
            jax.ShapeDtypeStruct((peers, local_slots, window), BF16),
            jax.ShapeDtypeStruct((all_rows, 1), jnp.int32),
        ),
        in_specs=[smem, vmem],
        compiler_params=params(),
        name="route",
    )(scal, x)
    arrived = lax.all_to_all(slots, "cols", 0, 0)
    x, place = lax.optimization_barrier((x, place))

    cols = min(512, width_d)
    part = (half, row_dev, width_d)
    keep, send = pl.pallas_call(
        functools.partial(base_kernel, plan),
        in_specs=[smem, vmem, anywhere],
        out_specs=(vmem, vmem),
        out_shape=(jax.ShapeDtypeStruct(part, F32), jax.ShapeDtypeStruct(part, BF16)),
        scratch_shapes=[
            pltpu.VMEM((all_rows, share), BF16),
            pltpu.VMEM((width_d // cols, share, cols), BF16),
            pltpu.SemaphoreType.DMA((width_d // cols,)),
        ],
        compiler_params=params(48),
        cost_estimate=pl.CostEstimate(
            flops=2 * all_rows * share * width_d,
            bytes_accessed=2 * share * width_d,
            transcendentals=0,
        ),
        name="base",
    )(scal, x, down_weight)
    pairs = lambda step: [(i, i ^ step) for i in range(peers)]
    base = pl.pallas_call(
        pair_kernel,
        out_shape=jax.ShapeDtypeStruct(keep.shape, F32),
        compiler_params=params(60),
        name="pair",
    )(keep, lax.ppermute(send, "cols", pairs(1)))
    base, arrived = lax.optimization_barrier((base, arrived))
    place = lax.dynamic_index_in_dim(place.reshape(half, 2, row_dev, 1), me % 2, 1, keepdims=False)
    place = place.reshape(half * row_dev, 1)

    group = split_factor(count, 64)
    shape = (local_slots, width_d)
    chunks = local_var * (count // group)
    deltas = pl.pallas_call(
        functools.partial(delta_kernel, plan, d_blocks, group),
        in_specs=[smem, vmem, anywhere],
        out_specs=vmem,
        scratch_shapes=[
            pltpu.VMEM((local_var, f_blocks, capacity, block_size), F32),
            pltpu.VMEM((local_var, d_blocks, capacity, block_size), F32),
            pltpu.VMEM((chunks, group, block_size, block_size), BF16),
            pltpu.SemaphoreType.DMA((chunks,)),
        ],
        out_shape=jax.ShapeDtypeStruct(shape, BF16),
        compiler_params=params(36),
        cost_estimate=pl.CostEstimate(
            flops=2 * local_slots * count * block_size * block_size,
            bytes_accessed=2 * local_var * count * block_size * block_size,
            transcendentals=0,
        ),
        name="delta",
    )(block_ids, arrived, delta_values)
    others = lax.ppermute(deltas, "cols", pairs(1))

    tile = width_d // 16
    above = [1 << k for k in range(1, peers.bit_length() - 1)]
    ends = []
    for side, order in enumerate((above, above[1:] + above[:1])):
        first, tiles = ((0, 11), (11, 16 - 11))[side]
        cols = tiles * tile
        open_bits = list(above)
        for count, step in enumerate(order):
            stride = 1 << open_bits.index(step)
            open_bits.remove(step)
            bit = ((me // step) % 2).astype(jnp.int32).reshape(1)
            left = (half >> (count + 1), row_dev, cols)
            outs = (jax.ShapeDtypeStruct(left, F32), jax.ShapeDtypeStruct(left, BF16))
            if count == 0:
                keep, send = pl.pallas_call(
                    functools.partial(join_kernel, stride, first * tile),
                    in_specs=[smem, smem, vmem, vmem, vmem, vmem],
                    out_shape=outs,
                    scratch_shapes=[pltpu.VMEM((half, row_dev, cols), F32)],
                    compiler_params=params(12),
                    name="join",
                )(scal, bit, base, place, deltas, others)
            else:
                keep, send = pl.pallas_call(
                    functools.partial(halve_kernel, stride),
                    in_specs=[smem, vmem, vmem],
                    out_shape=outs,
                    compiler_params=params(),
                    name="halve",
                )(bit, keep, got)
            got = lax.ppermute(send, "cols", pairs(step))
        ends += [keep, got]
    return pl.pallas_call(
        finish_kernel,
        out_shape=jax.ShapeDtypeStruct((row_dev, width_d), BF16),
        compiler_params=params(),
        name="finish",
    )(*ends)


def solution(mesh):
    return jax.shard_map(
        body,
        mesh=mesh,
        in_specs=(
            P(("groups", "cols"), None),
            P("cols", None),
            P("cols", None, None, None),
            P("cols", None),
            P(),
            P(("groups", "cols"), None),
        ),
        out_specs=P(("groups", "cols"), None),
        check_vma=False,
    )
```

```python
import functools
import math

import jax
import jax.numpy as jnp
from jax import lax
from jax.experimental import pallas as pl
from jax.experimental.pallas import tpu as pltpu
from jax.sharding import PartitionSpec as P

LANES = 128
BF16 = jnp.bfloat16
F32 = jnp.float32


def windows(width_f, peers):
    share = width_f // peers
    most = max((s * share) % LANES for s in range(peers))
    window = -(-(share + most) // LANES) * LANES
    if window == share:
        window += LANES
    last = (width_f - window) // LANES
    starts = [min(s * share // LANES, last) for s in range(peers)]
    return share, window, last, starts


def params(mib=16):
    return pltpu.CompilerParams(vmem_limit_bytes=mib * 1024 * 1024)


def lane_iota(rows, lanes):
    return lax.broadcasted_iota(jnp.int32, (rows, lanes), 1)


def split_kernel(
    plan, h_hbm, id_hbm, slot_hbm, o_hbm, h_ref, id_ref, slot_ref, o_ref, sems, out_sems
):
    share, window, _, starts = plan
    rows, width = h_ref.shape
    variants = slot_ref.shape[1]
    cut = width // LANES // 2 * LANES
    halves = (slice(0, cut), slice(cut, width))
    copies = [
        pltpu.make_async_copy(id_hbm, id_ref, sems.at[0]),
        pltpu.make_async_copy(slot_hbm, slot_ref, sems.at[1]),
        pltpu.make_async_copy(h_hbm.at[:, halves[0]], h_ref.at[:, halves[0]], sems.at[2]),
        pltpu.make_async_copy(h_hbm.at[:, halves[1]], h_ref.at[:, halves[1]], sems.at[3]),
    ]
    for copy in copies:
        copy.start()
    copies[0].wait()
    copies[1].wait()
    lane = lane_iota(rows, window)
    diagonal = lax.broadcasted_iota(jnp.int32, (rows, rows), 0) == lane_iota(rows, rows)
    ids = jnp.sum(jnp.where(diagonal, id_ref[...].astype(F32), 0.0), axis=1, keepdims=True)
    named = ids.astype(jnp.int32) == lane_iota(rows, variants)
    slot = jnp.sum(jnp.where(named, slot_ref[...].astype(F32), 0.0), axis=1, keepdims=True)
    copies[2].wait()
    late = True
    owners = len(starts) // out_sems.shape[0]
    done = []
    for s, b in enumerate(starts):
        if late and b * LANES + window > cut:
            copies[3].wait()
            late = False
        spare = (s * share - b * LANES + share) % window
        piece = h_ref[:, b * LANES : b * LANES + window].astype(F32)
        o_ref[s] = jnp.where(lane == spare, slot, piece).astype(BF16)
        if (s + 1) % owners == 0:
            at = pl.ds(s + 1 - owners, owners)
            done.append(
                pltpu.make_async_copy(o_ref.at[at], o_hbm.at[at], out_sems.at[s // owners])
            )
            done[-1].start()
    for copy in done:
        copy.wait()


def own_shift(plan):
    share, _, last, _ = plan
    start = lax.axis_index("cols") * share
    return start - jnp.minimum(start // LANES, last) * LANES


def route_kernel(plan, capacity, shift_ref, x_ref, o_hbm, place_ref, o_ref, sems):
    share, window, _, _ = plan
    peers, row_dev, _ = x_ref.shape
    rows = peers * row_dev
    slots = o_ref.shape[0] * o_ref.shape[1]
    variants = slots // capacity
    spare = lax.rem(shift_ref[0] + share, window)
    tile = pl.multiple_of(spare // LANES * LANES, LANES)
    near = x_ref[:, :, pl.ds(tile, LANES)].reshape(rows, LANES).astype(F32)
    at = lane_iota(rows, LANES) == spare - tile
    slot = jnp.sum(jnp.where(at, near, 0.0), axis=1, keepdims=True)
    data = x_ref[...].reshape(rows, window)
    onehot = jnp.where(slot.astype(jnp.int32) == lane_iota(rows, variants), 1.0, 0.0)
    row_i = lax.broadcasted_iota(jnp.int32, (rows, rows), 0)
    row_j = lane_iota(rows, rows)
    earlier = jnp.where(row_j < row_i, 1.0, 0.0).astype(BF16)
    before = jnp.dot(earlier, onehot.astype(BF16), preferred_element_type=F32)
    rank = jnp.sum(before * onehot, axis=1, keepdims=True)
    place = slot * capacity + rank
    place_ref[...] = place.astype(jnp.int32)
    across = jnp.sum(jnp.where(row_i == row_j, place, 0.0), axis=0, keepdims=True)
    across = across.astype(jnp.int32)
    parts = sems.shape[0]
    owners = peers // parts
    copies = []
    for p in range(parts):
        some = slots // parts
        named = lax.broadcasted_iota(jnp.int32, (some, rows), 0) + p * some
        pick = jnp.where(across == named, 1.0, 0.0).astype(BF16)
        filled = jnp.dot(pick, data, preferred_element_type=F32).astype(BF16)
        at = pl.ds(p * owners, owners)
        o_ref[at] = filled.reshape((owners,) + o_ref.shape[1:])
        copies.append(pltpu.make_async_copy(o_ref.at[at], o_hbm.at[at], sems.at[p]))
        copies[-1].start()
    for copy in copies:
        copy.wait()


def base_kernel(plan, scal_ref, x_ref, w_hbm, keep_ref, send_ref, mine_ref, w_ref, sems):
    share, window, _, _ = plan
    peers, row_dev, _ = x_ref.shape
    half = peers // 2 * row_dev
    parts, _, cols = w_ref.shape

    def fetch(p):
        return pltpu.make_async_copy(w_hbm.at[:, pl.ds(p * cols, cols)], w_ref.at[p], sems.at[p])

    for p in range(parts):
        fetch(p).start()
    bit = scal_ref[1]
    for side in (0, 1):
        which = bit if side == 0 else 1 - bit
        for q in range(peers // 2):
            piece = x_ref[2 * q + which].astype(F32)
            piece = pltpu.roll(piece, window - scal_ref[0], 1)
            at = side * half + q * row_dev
            mine_ref[at : at + row_dev] = piece[:, :share].astype(BF16)
    for p in range(parts):
        fetch(p).wait()
        both = jnp.dot(mine_ref[...], w_ref[p], preferred_element_type=F32)
        at = slice(p * cols, (p + 1) * cols)
        keep_ref[:, :, at] = both[:half].reshape(keep_ref.shape[:2] + (cols,))
        send_ref[:, :, at] = both[half:].astype(BF16).reshape(send_ref.shape[:2] + (cols,))


def delta_kernel(plan, d_blocks, group, ids_ref, x_ref, v_hbm, o_ref, rows_ref, acc_ref, held_ref, sems):
    share, window, _, starts = plan
    local_var, f_blocks, capacity, _ = rows_ref.shape
    chunks, _, size, _ = held_ref.shape
    per = chunks // local_var

    def fetch(c):
        source = v_hbm.at[c // per, pl.ds((c % per) * group, group)]
        return pltpu.make_async_copy(source, held_ref.at[c], sems.at[c])

    for c in range(chunks):
        fetch(c).start()

    acc_ref[...] = jnp.zeros_like(acc_ref)
    done = set()
    for s, b in enumerate(starts):
        for k in range(window // LANES):
            tile = x_ref[s, :, k * LANES : (k + 1) * LANES].astype(F32)
            low = s * share - (b + k) * LANES
            if low > 0 or low + share < LANES:
                lane = lane_iota(tile.shape[0], LANES)
                tile = jnp.where((lane >= low) & (lane < low + share), tile, 0.0)
            for v in range(local_var):
                part = tile[v * capacity : (v + 1) * capacity]
                if b + k in done:
                    part = part + rows_ref[v, b + k]
                rows_ref[v, b + k] = part
            done.add(b + k)

    zeros = jnp.zeros((capacity, size), F32)

    def one_chunk(c, carry):
        var = lax.div(c, per)
        first = lax.rem(c, per) * group
        pltpu.make_async_copy(
            v_hbm.at[var, pl.ds(first, group)], held_ref.at[c], sems.at[c]
        ).wait()
        sums = []
        for n in range(0, group, 2):
            blocks = [ids_ref[var, first + m] for m in range(n, min(n + 2, group))]
            lhs = [rows_ref[var, lax.div(block, d_blocks)] for block in blocks]
            if len(blocks) == 2:
                upper = jnp.concatenate([lhs[0], zeros], axis=1)
                lower = jnp.concatenate([zeros, lhs[1]], axis=1)
                left = jnp.concatenate([upper, lower], axis=0).astype(BF16)
                right = held_ref[c, n : n + 2].reshape(2 * size, size)
            else:
                left = lhs[0].astype(BF16)
                right = held_ref[c, n]
            product = jnp.dot(left, right, preferred_element_type=F32)
            for q, block in enumerate(blocks):
                part = product[q * capacity : (q + 1) * capacity]
                sums.append((lax.rem(block, d_blocks), part))
        for column, part in sums:
            acc_ref[var, column] += part
        return carry

    lax.fori_loop(0, chunks, one_chunk, 0)
    for j in range(d_blocks):
        whole = jnp.concatenate([acc_ref[v, j] for v in range(local_var)], axis=0)
        o_ref[:, j * LANES : (j + 1) * LANES] = whole.astype(BF16)


def pair_kernel(keep_ref, got_ref, o_ref):
    o_ref[...] = keep_ref[...] + got_ref[...].astype(F32)


def join_kernel(stride, first, scal_ref, bit_ref, base_ref, place_ref, own_ref, got_ref, *rest):
    next_ref, send_ref, sum_ref = rest
    rows = place_ref.shape[0]
    slots = own_ref.shape[0]
    cols = next_ref.shape[2]
    lane = lane_iota(rows, slots)
    picks = [place_ref[...] - scal_ref[k] == lane for k in (2, 3)]
    picks = [jnp.where(pick, 1.0, 0.0).astype(BF16) for pick in picks]
    step = math.gcd(cols, 512)
    for c in range(0, cols, step):
        at = slice(first + c, first + c + step)
        part = jnp.dot(picks[0], own_ref[:, at], preferred_element_type=F32)
        part += jnp.dot(picks[1], got_ref[:, at], preferred_element_type=F32)
        part = part.reshape(sum_ref.shape[:2] + (step,))
        sum_ref[:, :, c : c + step] = base_ref[:, :, at] + part
    bit = bit_ref[0]
    for q in range(next_ref.shape[0]):
        at = q // stride * 2 * stride + q % stride
        next_ref[q] = sum_ref[at + stride * bit]
        send_ref[q] = sum_ref[at + stride * (1 - bit)].astype(BF16)


def halve_kernel(stride, bit_ref, keep_ref, got_ref, next_ref, send_ref):
    bit = bit_ref[0]
    for q in range(next_ref.shape[0]):
        first = q // stride * 2 * stride + q % stride
        mine, other = first + stride * bit, first + stride * (1 - bit)
        next_ref[q] = keep_ref[mine] + got_ref[mine].astype(F32)
        send_ref[q] = (keep_ref[other] + got_ref[other].astype(F32)).astype(BF16)


def finish_kernel(*refs):
    o_ref = refs[-1]
    first = 0
    for side in (0, 1):
        keep_ref, got_ref = refs[2 * side : 2 * side + 2]
        cols = keep_ref.shape[2]
        total = keep_ref[0] + got_ref[0].astype(F32)
        o_ref[:, first : first + cols] = total.astype(BF16)
        first += cols


def split_factor(count, most):
    return max(g for g in range(1, most + 1) if count % g == 0)


def body(hidden, down_weight, delta_values, block_ids, variant_slot, row_variant):
    peers = lax.axis_size("cols")
    me = lax.axis_index("cols")
    row_dev, width_f = hidden.shape
    width_d = down_weight.shape[1]
    local_var, count, block_size, _ = delta_values.shape
    variants = variant_slot.shape[0]
    all_rows = row_dev * peers
    capacity = 2 * all_rows // variants
    d_blocks = width_d // block_size
    f_blocks = width_f // block_size
    local_slots = local_var * capacity
    plan = windows(width_f, peers)
    share, window, _, _ = plan
    half = peers // 2

    firsts = [me * local_slots, (me ^ 1) * local_slots]
    scal = jnp.stack([own_shift(plan), me % 2] + firsts).astype(jnp.int32)
    smem = pl.BlockSpec(memory_space=pltpu.SMEM)
    vmem = pl.BlockSpec(memory_space=pltpu.VMEM)
    anywhere = pl.BlockSpec(memory_space=pl.ANY)

    outgoing = pl.pallas_call(
        functools.partial(split_kernel, plan),
        in_specs=[anywhere] * 3,
        out_specs=anywhere,
        out_shape=jax.ShapeDtypeStruct((peers, row_dev, window), BF16),
        scratch_shapes=[
            pltpu.VMEM((row_dev, width_f), BF16),
            pltpu.VMEM((1, row_dev), jnp.int32),
            pltpu.VMEM((1, variants), jnp.int32),
            pltpu.VMEM((peers, row_dev, window), BF16),
            pltpu.SemaphoreType.DMA((4,)),
            pltpu.SemaphoreType.DMA((split_factor(peers, 4),)),
        ],
        compiler_params=params(60),
        name="split_rows",
    )(hidden, row_variant.reshape(1, row_dev), variant_slot.reshape(1, variants))
    x = lax.all_to_all(outgoing, "cols", 0, 0)

    slots, place = pl.pallas_call(
        functools.partial(route_kernel, plan, capacity),
        out_shape=(
            jax.ShapeDtypeStruct((peers, local_slots, window), BF16),
            jax.ShapeDtypeStruct((all_rows, 1), jnp.int32),
        ),
        in_specs=[smem, vmem],
        out_specs=(anywhere, vmem),
        scratch_shapes=[
            pltpu.VMEM((peers, local_slots, window), BF16),
            pltpu.SemaphoreType.DMA((split_factor(peers, 4),)),
        ],
        compiler_params=params(),
        name="route",
    )(scal, x)
    arrived = lax.all_to_all(slots, "cols", 0, 0)
    x, place = lax.optimization_barrier((x, place))

    cols = min(512, width_d)
    part = (half, row_dev, width_d)
    keep, send = pl.pallas_call(
        functools.partial(base_kernel, plan),
        in_specs=[smem, vmem, anywhere],
        out_specs=(vmem, vmem),
        out_shape=(jax.ShapeDtypeStruct(part, F32), jax.ShapeDtypeStruct(part, BF16)),
        scratch_shapes=[
            pltpu.VMEM((all_rows, share), BF16),
            pltpu.VMEM((width_d // cols, share, cols), BF16),
            pltpu.SemaphoreType.DMA((width_d // cols,)),
        ],
        compiler_params=params(48),
        cost_estimate=pl.CostEstimate(
            flops=2 * all_rows * share * width_d,
            bytes_accessed=2 * share * width_d,
            transcendentals=0,
        ),
        name="base",
    )(scal, x, down_weight)
    pairs = lambda step: [(i, i ^ step) for i in range(peers)]
    base = pl.pallas_call(
        pair_kernel,
        out_shape=jax.ShapeDtypeStruct(keep.shape, F32),
        compiler_params=params(60),
        name="pair",
    )(keep, lax.ppermute(send, "cols", pairs(1)))
    base, arrived = lax.optimization_barrier((base, arrived))
    place = lax.dynamic_index_in_dim(place.reshape(half, 2, row_dev, 1), me % 2, 1, keepdims=False)
    place = place.reshape(half * row_dev, 1)

    group = split_factor(count, 64)
    shape = (local_slots, width_d)
    chunks = local_var * (count // group)
    deltas = pl.pallas_call(
        functools.partial(delta_kernel, plan, d_blocks, group),
        in_specs=[smem, vmem, anywhere],
        out_specs=vmem,
        scratch_shapes=[
            pltpu.VMEM((local_var, f_blocks, capacity, block_size), F32),
            pltpu.VMEM((local_var, d_blocks, capacity, block_size), F32),
            pltpu.VMEM((chunks, group, block_size, block_size), BF16),
            pltpu.SemaphoreType.DMA((chunks,)),
        ],
        out_shape=jax.ShapeDtypeStruct(shape, BF16),
        compiler_params=params(36),
        cost_estimate=pl.CostEstimate(
            flops=2 * local_slots * count * block_size * block_size,
            bytes_accessed=2 * local_var * count * block_size * block_size,
            transcendentals=0,
        ),
        name="delta",
    )(block_ids, arrived, delta_values)
    others = lax.ppermute(deltas, "cols", pairs(1))

    tile = width_d // 16
    above = [1 << k for k in range(1, peers.bit_length() - 1)]
    ends = []
    for side, order in enumerate((above, above[1:] + above[:1])):
        first, tiles = ((0, 11), (11, 16 - 11))[side]
        cols = tiles * tile
        open_bits = list(above)
        for count, step in enumerate(order):
            stride = 1 << open_bits.index(step)
            open_bits.remove(step)
            bit = ((me // step) % 2).astype(jnp.int32).reshape(1)
            left = (half >> (count + 1), row_dev, cols)
            outs = (jax.ShapeDtypeStruct(left, F32), jax.ShapeDtypeStruct(left, BF16))
            if count == 0:
                keep, send = pl.pallas_call(
                    functools.partial(join_kernel, stride, first * tile),
                    in_specs=[smem, smem, vmem, vmem, vmem, vmem],
                    out_shape=outs,
                    scratch_shapes=[pltpu.VMEM((half, row_dev, cols), F32)],
                    compiler_params=params(12),
                    name="join",
                )(scal, bit, base, place, deltas, others)
            else:
                keep, send = pl.pallas_call(
                    functools.partial(halve_kernel, stride),
                    in_specs=[smem, vmem, vmem],
                    out_shape=outs,
                    compiler_params=params(),
                    name="halve",
                )(bit, keep, got)
            got = lax.ppermute(send, "cols", pairs(step))
        ends += [keep, got]
    return pl.pallas_call(
        finish_kernel,
        out_shape=jax.ShapeDtypeStruct((row_dev, width_d), BF16),
        compiler_params=params(),
        name="finish",
    )(*ends)


def solution(mesh):
    return jax.shard_map(
        body,
        mesh=mesh,
        in_specs=(
            P(("groups", "cols"), None),
            P("cols", None),
            P("cols", None, None, None),
            P("cols", None),
            P(),
            P(("groups", "cols"), None),
        ),
        out_specs=P(("groups", "cols"), None),
        check_vma=False,
    )
```

```python
import functools
import math

import jax
import jax.numpy as jnp
from jax import lax
from jax.experimental import pallas as pl
from jax.experimental.pallas import tpu as pltpu
from jax.sharding import PartitionSpec as P

LANES = 128
BF16 = jnp.bfloat16
F32 = jnp.float32


def windows(width_f, peers):
    share = width_f // peers
    most = max((s * share) % LANES for s in range(peers))
    window = -(-(share + most) // LANES) * LANES
    if window == share:
        window += LANES
    last = (width_f - window) // LANES
    starts = [min(s * share // LANES, last) for s in range(peers)]
    return share, window, last, starts


def params(mib=16):
    return pltpu.CompilerParams(vmem_limit_bytes=mib * 1024 * 1024)


def lane_iota(rows, lanes):
    return lax.broadcasted_iota(jnp.int32, (rows, lanes), 1)


def split_kernel(
    plan, h_hbm, id_hbm, slot_hbm, o_hbm, h_ref, id_ref, slot_ref, o_ref, sems, out_sems
):
    share, window, _, starts = plan
    rows, width = h_ref.shape
    variants = slot_ref.shape[1]
    cut = width // LANES // 2 * LANES
    halves = (slice(0, cut), slice(cut, width))
    copies = [
        pltpu.make_async_copy(id_hbm, id_ref, sems.at[0]),
        pltpu.make_async_copy(slot_hbm, slot_ref, sems.at[1]),
        pltpu.make_async_copy(h_hbm.at[:, halves[0]], h_ref.at[:, halves[0]], sems.at[2]),
        pltpu.make_async_copy(h_hbm.at[:, halves[1]], h_ref.at[:, halves[1]], sems.at[3]),
    ]
    for copy in copies:
        copy.start()
    copies[0].wait()
    copies[1].wait()
    lane = lane_iota(rows, window)
    diagonal = lax.broadcasted_iota(jnp.int32, (rows, rows), 0) == lane_iota(rows, rows)
    ids = jnp.sum(jnp.where(diagonal, id_ref[...].astype(F32), 0.0), axis=1, keepdims=True)
    named = ids.astype(jnp.int32) == lane_iota(rows, variants)
    slot = jnp.sum(jnp.where(named, slot_ref[...].astype(F32), 0.0), axis=1, keepdims=True)
    copies[2].wait()
    late = True
    owners = len(starts) // out_sems.shape[0]
    done = []
    for s, b in enumerate(starts):
        if late and b * LANES + window > cut:
            copies[3].wait()
            late = False
        spare = (s * share - b * LANES + share) % window
        piece = h_ref[:, b * LANES : b * LANES + window].astype(F32)
        o_ref[s] = jnp.where(lane == spare, slot, piece).astype(BF16)
        if (s + 1) % owners == 0:
            at = pl.ds(s + 1 - owners, owners)
            done.append(
                pltpu.make_async_copy(o_ref.at[at], o_hbm.at[at], out_sems.at[s // owners])
            )
            done[-1].start()
    for copy in done:
        copy.wait()


def own_shift(plan):
    share, _, last, _ = plan
    start = lax.axis_index("cols") * share
    return start - jnp.minimum(start // LANES, last) * LANES


def route_kernel(plan, capacity, shift_ref, x_ref, o_hbm, place_ref, o_ref, sems):
    share, window, _, _ = plan
    peers, row_dev, _ = x_ref.shape
    rows = peers * row_dev
    slots = o_ref.shape[0] * o_ref.shape[1]
    variants = slots // capacity
    spare = lax.rem(shift_ref[0] + share, window)
    tile = pl.multiple_of(spare // LANES * LANES, LANES)
    near = x_ref[:, :, pl.ds(tile, LANES)].reshape(rows, LANES).astype(F32)
    at = lane_iota(rows, LANES) == spare - tile
    slot = jnp.sum(jnp.where(at, near, 0.0), axis=1, keepdims=True)
    data = x_ref[...].reshape(rows, window)
    onehot = jnp.where(slot.astype(jnp.int32) == lane_iota(rows, variants), 1.0, 0.0)
    row_i = lax.broadcasted_iota(jnp.int32, (rows, rows), 0)
    row_j = lane_iota(rows, rows)
    earlier = jnp.where(row_j < row_i, 1.0, 0.0).astype(BF16)
    before = jnp.dot(earlier, onehot.astype(BF16), preferred_element_type=F32)
    rank = jnp.sum(before * onehot, axis=1, keepdims=True)
    place = slot * capacity + rank
    place_ref[...] = place.astype(jnp.int32)
    across = jnp.sum(jnp.where(row_i == row_j, place, 0.0), axis=0, keepdims=True)
    across = across.astype(jnp.int32)
    parts = sems.shape[0]
    owners = peers // parts
    copies = []
    for p in range(parts):
        some = slots // parts
        named = lax.broadcasted_iota(jnp.int32, (some, rows), 0) + p * some
        pick = jnp.where(across == named, 1.0, 0.0).astype(BF16)
        filled = jnp.dot(pick, data, preferred_element_type=F32).astype(BF16)
        at = pl.ds(p * owners, owners)
        o_ref[at] = filled.reshape((owners,) + o_ref.shape[1:])
        copies.append(pltpu.make_async_copy(o_ref.at[at], o_hbm.at[at], sems.at[p]))
        copies[-1].start()
    for copy in copies:
        copy.wait()


def base_kernel(plan, scal_ref, x_ref, w_hbm, keep_ref, send_ref, mine_ref, w_ref, sems):
    share, window, _, _ = plan
    peers, row_dev, _ = x_ref.shape
    half = peers // 2 * row_dev
    parts, _, cols = w_ref.shape

    def fetch(p):
        return pltpu.make_async_copy(w_hbm.at[:, pl.ds(p * cols, cols)], w_ref.at[p], sems.at[p])

    for p in range(parts):
        fetch(p).start()
    bit = scal_ref[1]
    for side in (0, 1):
        which = bit if side == 0 else 1 - bit
        for q in range(peers // 2):
            piece = x_ref[2 * q + which].astype(F32)
            piece = pltpu.roll(piece, window - scal_ref[0], 1)
            at = side * half + q * row_dev
            mine_ref[at : at + row_dev] = piece[:, :share].astype(BF16)
    for p in range(parts):
        fetch(p).wait()
        both = jnp.dot(mine_ref[...], w_ref[p], preferred_element_type=F32)
        at = slice(p * cols, (p + 1) * cols)
        keep_ref[:, :, at] = both[:half].reshape(keep_ref.shape[:2] + (cols,))
        send_ref[:, :, at] = both[half:].astype(BF16).reshape(send_ref.shape[:2] + (cols,))


def delta_kernel(plan, d_blocks, group, ids_ref, x_ref, v_hbm, o_ref, rows_ref, acc_ref, held_ref, sems):
    share, window, _, starts = plan
    local_var, f_blocks, capacity, _ = rows_ref.shape
    chunks, _, size, _ = held_ref.shape
    per = chunks // local_var

    def fetch(c):
        source = v_hbm.at[c // per, pl.ds((c % per) * group, group)]
        return pltpu.make_async_copy(source, held_ref.at[c], sems.at[c])

    for c in range(chunks):
        fetch(c).start()

    acc_ref[...] = jnp.zeros_like(acc_ref)
    done = set()
    for s, b in enumerate(starts):
        for k in range(window // LANES):
            tile = x_ref[s, :, k * LANES : (k + 1) * LANES].astype(F32)
            low = s * share - (b + k) * LANES
            if low > 0 or low + share < LANES:
                lane = lane_iota(tile.shape[0], LANES)
                tile = jnp.where((lane >= low) & (lane < low + share), tile, 0.0)
            for v in range(local_var):
                part = tile[v * capacity : (v + 1) * capacity]
                if b + k in done:
                    part = part + rows_ref[v, b + k]
                rows_ref[v, b + k] = part
            done.add(b + k)

    zeros = jnp.zeros((capacity, size), F32)

    def one_chunk(c, carry):
        var = lax.div(c, per)
        first = lax.rem(c, per) * group
        pltpu.make_async_copy(
            v_hbm.at[var, pl.ds(first, group)], held_ref.at[c], sems.at[c]
        ).wait()
        sums = []
        for n in range(0, group, 2):
            blocks = [ids_ref[var, first + m] for m in range(n, min(n + 2, group))]
            lhs = [rows_ref[var, lax.div(block, d_blocks)] for block in blocks]
            if len(blocks) == 2:
                upper = jnp.concatenate([lhs[0], zeros], axis=1)
                lower = jnp.concatenate([zeros, lhs[1]], axis=1)
                left = jnp.concatenate([upper, lower], axis=0).astype(BF16)
                right = held_ref[c, n : n + 2].reshape(2 * size, size)
            else:
                left = lhs[0].astype(BF16)
                right = held_ref[c, n]
            product = jnp.dot(left, right, preferred_element_type=F32)
            for q, block in enumerate(blocks):
                part = product[q * capacity : (q + 1) * capacity]
                sums.append((lax.rem(block, d_blocks), part))
        for column, part in sums:
            acc_ref[var, column] += part
        return carry

    lax.fori_loop(0, chunks, one_chunk, 0)
    for j in range(d_blocks):
        whole = jnp.concatenate([acc_ref[v, j] for v in range(local_var)], axis=0)
        o_ref[:, j * LANES : (j + 1) * LANES] = whole.astype(BF16)


def pair_kernel(keep_ref, got_ref, o_ref):
    o_ref[...] = keep_ref[...] + got_ref[...].astype(F32)


def join_kernel(stride, first, scal_ref, bit_ref, base_ref, place_ref, own_ref, got_ref, *rest):
    next_ref, send_ref, sum_ref = rest
    rows = place_ref.shape[0]
    slots = own_ref.shape[0]
    cols = next_ref.shape[2]
    lane = lane_iota(rows, slots)
    picks = [place_ref[...] - scal_ref[k] == lane for k in (2, 3)]
    picks = [jnp.where(pick, 1.0, 0.0).astype(BF16) for pick in picks]
    step = math.gcd(cols, 512)
    for c in range(0, cols, step):
        at = slice(first + c, first + c + step)
        part = jnp.dot(picks[0], own_ref[:, at], preferred_element_type=F32)
        part += jnp.dot(picks[1], got_ref[:, at], preferred_element_type=F32)
        part = part.reshape(sum_ref.shape[:2] + (step,))
        sum_ref[:, :, c : c + step] = base_ref[:, :, at] + part
    bit = bit_ref[0]
    for q in range(next_ref.shape[0]):
        at = q // stride * 2 * stride + q % stride
        next_ref[q] = sum_ref[at + stride * bit]
        send_ref[q] = sum_ref[at + stride * (1 - bit)].astype(BF16)


def halve_kernel(stride, bit_ref, keep_ref, got_ref, next_ref, send_ref):
    bit = bit_ref[0]
    for q in range(next_ref.shape[0]):
        first = q // stride * 2 * stride + q % stride
        mine, other = first + stride * bit, first + stride * (1 - bit)
        next_ref[q] = keep_ref[mine] + got_ref[mine].astype(F32)
        send_ref[q] = (keep_ref[other] + got_ref[other].astype(F32)).astype(BF16)


def finish_kernel(*refs):
    o_ref = refs[-1]
    first = 0
    for side in (0, 1):
        keep_ref, got_ref = refs[2 * side : 2 * side + 2]
        cols = keep_ref.shape[2]
        total = keep_ref[0] + got_ref[0].astype(F32)
        o_ref[:, first : first + cols] = total.astype(BF16)
        first += cols


def split_factor(count, most):
    return max(g for g in range(1, most + 1) if count % g == 0)


def body(hidden, down_weight, delta_values, block_ids, variant_slot, row_variant):
    peers = lax.axis_size("cols")
    me = lax.axis_index("cols")
    row_dev, width_f = hidden.shape
    width_d = down_weight.shape[1]
    local_var, count, block_size, _ = delta_values.shape
    variants = variant_slot.shape[0]
    all_rows = row_dev * peers
    capacity = 2 * all_rows // variants
    d_blocks = width_d // block_size
    f_blocks = width_f // block_size
    local_slots = local_var * capacity
    plan = windows(width_f, peers)
    share, window, _, _ = plan
    half = peers // 2

    firsts = [me * local_slots, (me ^ 1) * local_slots]
    scal = jnp.stack([own_shift(plan), me % 2] + firsts).astype(jnp.int32)
    smem = pl.BlockSpec(memory_space=pltpu.SMEM)
    vmem = pl.BlockSpec(memory_space=pltpu.VMEM)
    anywhere = pl.BlockSpec(memory_space=pl.ANY)

    outgoing = pl.pallas_call(
        functools.partial(split_kernel, plan),
        in_specs=[anywhere] * 3,
        out_specs=anywhere,
        out_shape=jax.ShapeDtypeStruct((peers, row_dev, window), BF16),
        scratch_shapes=[
            pltpu.VMEM((row_dev, width_f), BF16),
            pltpu.VMEM((1, row_dev), jnp.int32),
            pltpu.VMEM((1, variants), jnp.int32),
            pltpu.VMEM((peers, row_dev, window), BF16),
            pltpu.SemaphoreType.DMA((4,)),
            pltpu.SemaphoreType.DMA((split_factor(peers, 4),)),
        ],
        compiler_params=params(60),
        name="split_rows",
    )(hidden, row_variant.reshape(1, row_dev), variant_slot.reshape(1, variants))
    x = lax.all_to_all(outgoing, "cols", 0, 0)

    slots, place = pl.pallas_call(
        functools.partial(route_kernel, plan, capacity),
        out_shape=(
            jax.ShapeDtypeStruct((peers, local_slots, window), BF16),
            jax.ShapeDtypeStruct((all_rows, 1), jnp.int32),
        ),
        in_specs=[smem, vmem],
        out_specs=(anywhere, vmem),
        scratch_shapes=[
            pltpu.VMEM((peers, local_slots, window), BF16),
            pltpu.SemaphoreType.DMA((split_factor(peers, 4),)),
        ],
        compiler_params=params(),
        name="route",
    )(scal, x)
    arrived = lax.all_to_all(slots, "cols", 0, 0)
    x, place = lax.optimization_barrier((x, place))

    cols = min(512, width_d)
    part = (half, row_dev, width_d)
    keep, send = pl.pallas_call(
        functools.partial(base_kernel, plan),
        in_specs=[smem, vmem, anywhere],
        out_specs=(vmem, vmem),
        out_shape=(jax.ShapeDtypeStruct(part, F32), jax.ShapeDtypeStruct(part, BF16)),
        scratch_shapes=[
            pltpu.VMEM((all_rows, share), BF16),
            pltpu.VMEM((width_d // cols, share, cols), BF16),
            pltpu.SemaphoreType.DMA((width_d // cols,)),
        ],
        compiler_params=params(48),
        cost_estimate=pl.CostEstimate(
            flops=2 * all_rows * share * width_d,
            bytes_accessed=2 * share * width_d,
            transcendentals=0,
        ),
        name="base",
    )(scal, x, down_weight)
    pairs = lambda step: [(i, i ^ step) for i in range(peers)]
    base = pl.pallas_call(
        pair_kernel,
        out_shape=jax.ShapeDtypeStruct(keep.shape, F32),
        compiler_params=params(60),
        name="pair",
    )(keep, lax.ppermute(send, "cols", pairs(1)))
    base, arrived = lax.optimization_barrier((base, arrived))
    place = lax.dynamic_index_in_dim(place.reshape(half, 2, row_dev, 1), me % 2, 1, keepdims=False)
    place = place.reshape(half * row_dev, 1)

    group = split_factor(count, 64)
    shape = (local_slots, width_d)
    chunks = local_var * (count // group)
    deltas = pl.pallas_call(
        functools.partial(delta_kernel, plan, d_blocks, group),
        in_specs=[smem, vmem, anywhere],
        out_specs=vmem,
        scratch_shapes=[
            pltpu.VMEM((local_var, f_blocks, capacity, block_size), F32),
            pltpu.VMEM((local_var, d_blocks, capacity, block_size), F32),
            pltpu.VMEM((chunks, group, block_size, block_size), BF16),
            pltpu.SemaphoreType.DMA((chunks,)),
        ],
        out_shape=jax.ShapeDtypeStruct(shape, BF16),
        compiler_params=params(36),
        cost_estimate=pl.CostEstimate(
            flops=2 * local_slots * count * block_size * block_size,
            bytes_accessed=2 * local_var * count * block_size * block_size,
            transcendentals=0,
        ),
        name="delta",
    )(block_ids, arrived, delta_values)
    others = lax.ppermute(deltas, "cols", pairs(1))

    tile = width_d // 32
    above = [1 << k for k in range(1, peers.bit_length() - 1)]
    ends = []
    for side, order in enumerate((above, above[1:] + above[:1])):
        first, tiles = ((0, 21), (21, 32 - 21))[side]
        cols = tiles * tile
        open_bits = list(above)
        for count, step in enumerate(order):
            stride = 1 << open_bits.index(step)
            open_bits.remove(step)
            bit = ((me // step) % 2).astype(jnp.int32).reshape(1)
            left = (half >> (count + 1), row_dev, cols)
            outs = (jax.ShapeDtypeStruct(left, F32), jax.ShapeDtypeStruct(left, BF16))
            if count == 0:
                keep, send = pl.pallas_call(
                    functools.partial(join_kernel, stride, first * tile),
                    in_specs=[smem, smem, vmem, vmem, vmem, vmem],
                    out_shape=outs,
                    scratch_shapes=[pltpu.VMEM((half, row_dev, cols), F32)],
                    compiler_params=params(12),
                    name="join",
                )(scal, bit, base, place, deltas, others)
            else:
                keep, send = pl.pallas_call(
                    functools.partial(halve_kernel, stride),
                    in_specs=[smem, vmem, vmem],
                    out_shape=outs,
                    compiler_params=params(),
                    name="halve",
                )(bit, keep, got)
            got = lax.ppermute(send, "cols", pairs(step))
        ends += [keep, got]
    return pl.pallas_call(
        finish_kernel,
        out_shape=jax.ShapeDtypeStruct((row_dev, width_d), BF16),
        compiler_params=params(),
        name="finish",
    )(*ends)


def solution(mesh):
    return jax.shard_map(
        body,
        mesh=mesh,
        in_specs=(
            P(("groups", "cols"), None),
            P("cols", None),
            P("cols", None, None, None),
            P("cols", None),
            P(),
            P(("groups", "cols"), None),
        ),
        out_specs=P(("groups", "cols"), None),
        check_vma=False,
    )
```
